32 devices in a mesh: groups: 2 (over x), dp: 8 (over z, y), tensor: 2 (over core).
Axes of the slice: x: 2, y: 2, z: 4, core: 2. Of those that a mesh axis runs over, the one named last changes fastest.
Arguments:
- step_input: bfloat16 [1024, 4, 8192], P(('groups', 'dp'), None, 'tensor'), parts along dimension 0, may hold values from -8 to 8
- new_kv: bfloat16 [1024, 4, 2, 1024], P(('groups', 'dp'), None, None, 'tensor'), parts along dimension 0, may hold values from -24 to 24
- resp_cache: bfloat16 [1024, 8, 2, 1024], P(('groups', 'dp'), None, None, 'tensor'), parts along dimension 0, may hold values from -24 to 24
- policy_prompt: bfloat16 [16, 128, 2, 1024], P(('groups', 'dp'), None, None, 'tensor'), parts along dimension 0, may hold values from -24 to 24
- ref_prompt: bfloat16 [16, 128, 2, 1024], P(('groups', 'dp'), None, None, 'tensor'), parts along dimension 0, may hold values from -24 to 24
- prompt_len: int32 [16], P(('groups', 'dp')), parts along dimension 0, may hold values from 1 to 128
- resp_len: int32 [1024], P(('groups', 'dp')), parts along dimension 0, may hold values from 1 to 8
- row_owner: int32 [1024], P(('groups', 'dp')), parts along dimension 0, may hold values from 0 to 7, as said below
- finished: int32 [1024], P(('groups', 'dp')), parts along dimension 0, may hold values 0 or 1
- probe: float32 [8192], P('tensor'), may hold values from -0.12 to 0.12
Outputs:
- decoded: bfloat16 [1024, 4, 8192], P(('groups', 'dp'), None, 'tensor'), parts along dimension 0
- ref_score: float32 [16, 64, 4], P(('groups', 'dp')), parts along dimension 0
The draws below stay inside these ranges and needn't reach their ends.
There are 2 independent parts, one for each index of `groups`. The reference program is written for one: setup_inputs(seed, part) draws one part's arguments, and reference() takes and returns one part's arrays. A program takes and returns all parts, laid end to end along the dimension named above; an argument that names none is the same for every part. Nothing has to cross between parts.
Inputs may be any that keep to these rules, and one draw needn't show every extreme that they name: `row_owner`: among the rows of one block at most 8 name the same owner; in every draw one owner is named by exactly 8 rows of every block.
All inputs are finite; a program needn't handle non-finite values. No bound on the sum of `finished` on one device may be relied on, other than what follows from the above.
Results may differ from the reference program's by a relative error of at most 0.012.
The reference program's roundings to bfloat16 on the way count: a program that leaves them out, or rounds other values in their place, can miss the bound.
Values may be sent and summed in bfloat16 or wider, within the bound.
A program may use at most 128 MiB of HBM per device.

```python
import math
from functools import partial
import jax
import jax.numpy as jnp
from jax import lax

HQ = 64
KVH = 8
HD = 128
ROWS_DEV = 64
PL = 128
RL = 8
S = 4
CAP = 8
ROWS = 512
N_DP = 8


def kv_block(key, lead_shape, length, salt):
    own_key = jax.random.fold_in(key, salt)
    first_key, second_key = jax.random.split(own_key, 2)
    full_shape = lead_shape + (length, KVH * HD)
    keys_part = jnp.clip(jax.random.normal(first_key, full_shape), -6.0, 6.0)
    values_part = 4.0 * jnp.clip(jax.random.normal(second_key, full_shape), -6.0, 6.0)
    return jnp.stack([keys_part, values_part], axis=-2).astype(jnp.float32)


def draw_policy_prompt(key, part):
    return kv_block(key, (N_DP,), PL, 101).astype(jnp.bfloat16)


def draw_ref_prompt(key, part):
    return kv_block(key, (N_DP,), PL, 102).astype(jnp.bfloat16)


def draw_resp_cache(key, part):
    return kv_block(key, (ROWS_DEV * N_DP,), RL, 103).astype(jnp.bfloat16)


def draw_new_kv(key, part):
    return kv_block(key, (ROWS_DEV * N_DP,), S, 104).astype(jnp.bfloat16)


def draw_step_input(key, part):
    own_key = jax.random.fold_in(key, 105)
    full_shape = (ROWS_DEV * N_DP, S, HQ * HD)
    return jnp.clip(jax.random.normal(own_key, full_shape), -8.0, 8.0).astype(jnp.bfloat16)


def draw_row_owner(key, part):
    own_key = jax.random.fold_in(key, 106)
    busiest = jax.random.randint(jax.random.fold_in(own_key, 1), (), 0, N_DP)
    others = (busiest + 1 + jnp.arange((N_DP - 1) * CAP) // CAP) % N_DP

    def one_block(block_id):
        block_key = jax.random.fold_in(own_key, block_id + 2)
        first_key, second_key = jax.random.split(block_key)
        picked = jax.random.permutation(first_key, others)[:ROWS_DEV - CAP]
        owners = jnp.concatenate([jnp.full((CAP,), busiest, jnp.int32), picked.astype(jnp.int32)])
        return jax.random.permutation(second_key, owners)
    return jax.vmap(one_block)(jnp.arange(N_DP)).reshape(ROWS_DEV * N_DP).astype(jnp.int32)


def draw_resp_len(key, part):
    own_key = jax.random.fold_in(key, 107)
    first_key, second_key = jax.random.split(own_key)
    lengths = jax.random.randint(first_key, (ROWS_DEV * N_DP,), 1, RL + 1)
    longest = jax.random.randint(second_key, (), 0, ROWS_DEV * N_DP)
    return jnp.where(jnp.arange(ROWS_DEV * N_DP) == longest, RL, lengths).astype(jnp.int32)


def draw_prompt_len(key, part):
    own_key = jax.random.fold_in(key, 108)
    first_key, second_key = jax.random.split(own_key)
    lengths = jax.random.randint(first_key, (N_DP,), 1, PL + 1)
    longest = jax.random.randint(second_key, (), 0, N_DP)
    return jnp.where(jnp.arange(N_DP) == longest, PL, lengths).astype(jnp.int32)


def touch_ends(drawn, rng, smallest, high):
    longest = drawn.shape.index(max(drawn.shape))
    spots = []
    for shift in (0, 1):
        where = [jax.random.randint(jax.random.fold_in(rng, axis), (), 0, length) for axis, length in enumerate(drawn.shape)]
        where[longest] = (where[longest] + shift) % drawn.shape[longest]
        spots.append(tuple(where))
    return drawn.at[spots[0]].set(smallest).at[spots[1]].set(high)


def block_scale(stream_key, extent, shards, smallest, top_value):
    def one(dim, parts):
        heights = jax.random.uniform(jax.random.fold_in(jax.random.fold_in(stream_key, 6), dim), (parts,), jnp.float32, smallest / len(shards), top_value / len(shards))
        return jnp.repeat(jnp.exp(heights), extent[dim] // parts).reshape((-1,) + (1,) * (len(extent) - dim - 1))

    level = one(*shards[0])
    for cut in shards[1:]:
        level = level * one(*cut)
    return level


def centred(stream_key, extent, width, reach, cuts=(), held_as=jnp.bfloat16):
    array = width * jax.random.normal(stream_key, extent, jnp.float32)
    if cuts:
        array = array * block_scale(stream_key, extent, cuts, -0.22, 0.18)
    return jnp.clip(array, -reach, reach).astype(held_as)


def setup_inputs(seed: int = 0, part: int = 0) -> dict:
    seeds = jax.random.split(jax.random.key(seed), 11)
    part_keys = jax.random.split(jax.random.fold_in(seeds[10], part), 11)
    return {
        "step_input": draw_step_input(jax.random.fold_in(jax.random.fold_in(seeds[10], part), 71), part),
        "new_kv": draw_new_kv(jax.random.fold_in(jax.random.fold_in(seeds[10], part), 71), part),
        "resp_cache": draw_resp_cache(jax.random.fold_in(jax.random.fold_in(seeds[10], part), 71), part),
        "policy_prompt": draw_policy_prompt(jax.random.fold_in(jax.random.fold_in(seeds[10], part), 71), part),
        "ref_prompt": draw_ref_prompt(jax.random.fold_in(jax.random.fold_in(seeds[10], part), 71), part),
        "prompt_len": draw_prompt_len(jax.random.fold_in(jax.random.fold_in(seeds[10], part), 71), part),
        "resp_len": draw_resp_len(jax.random.fold_in(jax.random.fold_in(seeds[10], part), 71), part),
        "row_owner": draw_row_owner(jax.random.fold_in(jax.random.fold_in(seeds[10], part), 71), part),
        "finished": touch_ends((jax.random.randint(part_keys[8], (ROWS,), 0, 4) < 3).astype(jnp.int32), jax.random.fold_in(part_keys[8], 1), 0, 1),
        "probe": centred(seeds[9], (HQ * HD,), 0.02, 0.12, ((0, 2),), jnp.float32),
    }


def softmax_pieces(scores, key_valid):
    masked = jnp.where(key_valid, scores, -jnp.inf)
    top_score = lax.optimization_barrier(jnp.max(masked, axis=-1, keepdims=True))
    weight = jnp.exp(masked - top_score)
    return (weight, lax.optimization_barrier(jnp.sum(weight, axis=-1)), top_score[..., 0])

def slot_table(row_owner):
    row_count = ROWS_DEV * N_DP
    slot_count = N_DP * CAP
    blocks = row_owner.reshape(N_DP, ROWS_DEV)
    local_iota = jnp.arange(ROWS_DEV)
    earlier = local_iota[None, :] < local_iota[:, None]
    same_owner = (blocks[:, :, None] == blocks[:, None, :]) & earlier[None]
    row_rank = lax.optimization_barrier(jnp.sum(same_owner.astype(jnp.int32), axis=2)).reshape(row_count)
    source = (jnp.arange(row_count) // ROWS_DEV).astype(jnp.int32)
    flat_slot = (row_owner * slot_count + source * CAP + row_rank).astype(jnp.int32)
    table = jnp.full((N_DP * slot_count,), row_count, jnp.int32)
    table = table.at[flat_slot].set(jnp.arange(row_count).astype(jnp.int32))
    return (flat_slot, table.reshape(N_DP, slot_count))

def reference(step_input, new_kv, resp_cache, policy_prompt, ref_prompt, prompt_len, resp_len, row_owner, finished, probe):
    row_count = ROWS_DEV * N_DP
    slot_count = N_DP * CAP
    group_size = HQ // KVH
    q_width = HQ * HD
    kv_width = KVH * HD
    inv_scale = 1.0 / math.sqrt(HD)
    flat_slot, row_of_slot = slot_table(row_owner)
    safe_rows = jnp.minimum(row_of_slot, row_count - 1)
    slot_used = row_of_slot < row_count
    prompt_iota = jnp.arange(PL)
    reply_iota = jnp.arange(RL + S)
    own_all = jnp.concatenate([resp_cache, new_kv], axis=1)
    blocked_all = own_all.reshape(N_DP, ROWS_DEV, RL + S, 2, kv_width)
    blocked_len = resp_len.reshape(N_DP, ROWS_DEV)

    def prompt_part(packed):
        queries, cache_rows, length = packed
        query_heads = queries.astype(jnp.float32).reshape(slot_count, KVH, group_size, HD)
        prompt_keys = cache_rows[:, 0].astype(jnp.float32).reshape(PL, KVH, HD)
        prompt_values = cache_rows[:, 1].astype(jnp.float32).reshape(PL, KVH, HD)
        scores = jnp.einsum('skgd,tkd->skgt', query_heads, prompt_keys) * inv_scale
        weight, weight_sum, top_score = softmax_pieces(scores, prompt_iota < length)
        weight_low = lax.optimization_barrier(weight.astype(jnp.bfloat16)).astype(jnp.float32)
        summed = jnp.einsum('skgt,tkd->skgd', weight_low, prompt_values)
        part_out = (summed / weight_sum[..., None]).astype(jnp.bfloat16).reshape(slot_count, q_width)
        part_lse = (top_score + jnp.log(weight_sum)).reshape(slot_count, HQ)
        return (part_out, part_lse)

    def own_part(step_idx, packed):
        queries, cache_rows, lengths = packed
        query_heads = queries.astype(jnp.float32).reshape(ROWS_DEV, KVH, group_size, HD)
        reply_keys = cache_rows[:, :, 0].astype(jnp.float32).reshape(ROWS_DEV, RL + S, KVH, HD)
        reply_values = cache_rows[:, :, 1].astype(jnp.float32).reshape(ROWS_DEV, RL + S, KVH, HD)
        scores = jnp.einsum('rkgd,rtkd->rkgt', query_heads, reply_keys) * inv_scale
        reply_valid = jnp.where(reply_iota[None, :] < RL, reply_iota[None, :] < lengths[:, None], reply_iota[None, :] <= RL + step_idx)
        weight, weight_sum, top_score = softmax_pieces(scores, reply_valid[:, None, None, :])
        weight_low = lax.optimization_barrier(weight.astype(jnp.bfloat16)).astype(jnp.float32)
        summed = jnp.einsum('rkgt,rtkd->rkgd', weight_low, reply_values)
        own_out = (summed / weight_sum[..., None]).reshape(ROWS_DEV, q_width)
        own_lse = (top_score + jnp.log(weight_sum)).reshape(ROWS_DEV, HQ)
        return (own_out, own_lse)
    previous = jnp.zeros((row_count, q_width), jnp.float32)
    decoded_list = []
    query_list = []
    for step_idx in range(S):
        queries = (step_input[:, step_idx].astype(jnp.float32) + previous).astype(jnp.bfloat16)
        query_list.append(queries)
        slot_queries = jnp.where(slot_used[:, :, None], jnp.take(queries, safe_rows, axis=0), jnp.zeros((), jnp.bfloat16))
        part_out, part_lse = lax.map(prompt_part, (slot_queries, policy_prompt, prompt_len))
        prompt_out = jnp.take(part_out.reshape(N_DP * slot_count, q_width), flat_slot, axis=0).astype(jnp.float32)
        prompt_lse = jnp.take(part_lse.reshape(N_DP * slot_count, HQ), flat_slot, axis=0)
        own_out, own_lse = lax.map(partial(own_part, step_idx), (queries.reshape(N_DP, ROWS_DEV, q_width), blocked_all, blocked_len))
        own_out = own_out.reshape(row_count, HQ, HD)
        own_lse = own_lse.reshape(row_count, HQ)
        joint_lse = jnp.maximum(prompt_lse, own_lse)
        prompt_wt = jnp.exp(prompt_lse - joint_lse)
        own_wt = jnp.exp(own_lse - joint_lse)
        blended = (prompt_wt[..., None] * prompt_out.reshape(row_count, HQ, HD) + own_wt[..., None] * own_out) / (prompt_wt + own_wt)[..., None]
        decoded_now = blended.reshape(row_count, q_width).astype(jnp.bfloat16)
        decoded_list.append(decoded_now)
        previous = lax.optimization_barrier(decoded_now).astype(jnp.float32)
    query_all = jnp.stack(query_list, axis=1)
    live_len = jnp.where(finished == 1, resp_len, 0).astype(jnp.int32)
    probe_heads = probe.reshape(KVH, group_size, HD)

    def score_owner(packed):
        slot_rows, used, cache_rows, length = packed
        slot_len = jnp.where(used, jnp.take(live_len, slot_rows), 0)
        slot_kv = jnp.take(own_all, slot_rows, axis=0).astype(jnp.float32)
        slot_keys = slot_kv[:, :, 0].reshape(slot_count, RL + S, KVH, HD)
        slot_values = slot_kv[:, :, 1].reshape(slot_count, RL + S, KVH, HD)
        slot_queries = jnp.take(query_all, slot_rows, axis=0)
        prompt_keys = cache_rows[:, 0].astype(jnp.float32).reshape(PL, KVH, HD)
        prompt_values = cache_rows[:, 1].astype(jnp.float32).reshape(PL, KVH, HD)
        prompt_valid = jnp.broadcast_to((prompt_iota < length)[None, :], (slot_count, PL))
        columns = []
        for step_idx in range(S):
            query_heads = slot_queries[:, step_idx].astype(jnp.float32).reshape(slot_count, KVH, group_size, HD)
            prompt_scores = jnp.einsum('skgd,tkd->skgt', query_heads, prompt_keys) * inv_scale
            reply_scores = jnp.einsum('skgd,stkd->skgt', query_heads, slot_keys) * inv_scale
            reply_valid = jnp.where(reply_iota[None, :] < RL, reply_iota[None, :] < slot_len[:, None], reply_iota[None, :] <= RL + step_idx)
            key_valid = jnp.concatenate([prompt_valid, reply_valid], axis=1)
            weight, weight_sum, top_score = softmax_pieces(jnp.concatenate([prompt_scores, reply_scores], axis=-1), key_valid[:, None, None, :])
            weight_low = lax.optimization_barrier(weight.astype(jnp.bfloat16)).astype(jnp.float32)
            summed = jnp.einsum('skgt,tkd->skgd', weight_low[..., :PL], prompt_values)
            summed = summed + jnp.einsum('skgt,stkd->skgd', weight_low[..., PL:], slot_values)
            ref_out = summed / weight_sum[..., None]
            columns.append(jnp.einsum('skgd,kgd->s', ref_out, probe_heads, precision=lax.Precision.HIGHEST))
        stacked = jnp.stack(columns, axis=1)
        return jnp.where(slot_len[:, None] > 0, stacked, jnp.zeros((), jnp.float32))
    ref_score = lax.map(score_owner, (safe_rows, slot_used, ref_prompt, prompt_len))
    return (jnp.stack(decoded_list, axis=1), ref_score)
```

```python
import functools
import math

import jax
import jax.numpy as jnp
from jax import lax
from jax.experimental import pallas as pl
from jax.experimental.pallas import tpu as pltpu
from jax.sharding import PartitionSpec as P

HD = 128
LOG2E = 1.4426950408889634


def softmax_pieces(scores, key_valid):
    masked = jnp.where(key_valid, scores, -jnp.inf)
    top_score = jnp.max(masked, axis=-1, keepdims=True)
    weight = jnp.exp(masked - top_score)
    return (weight, jnp.sum(weight, axis=-1), top_score[..., 0])


def per_device_routed(
    step_input,
    new_kv,
    resp_cache,
    policy_prompt,
    ref_prompt,
    prompt_len,
    resp_len,
    row_owner,
    finished,
    probe,
):
    row_count = step_input.shape[0]
    step_count = step_input.shape[1]
    q_width = step_input.shape[2]
    kv_width = new_kv.shape[3]
    q_heads = q_width // HD
    kv_heads = kv_width // HD
    group_size = q_heads // kv_heads
    inv_scale = 1.0 / math.sqrt(HD)
    peer_count = lax.axis_size("dp")
    capacity = max(2, (row_count + peer_count - 1) // peer_count)
    slot_count = peer_count * capacity
    resp_slots = resp_cache.shape[1]
    prompt_width = policy_prompt.shape[1]
    row_iota = jnp.arange(row_count, dtype=jnp.int32)
    same_owner = (row_owner[:, None] == row_owner[None, :]) & (
        row_iota[None, :] < row_iota[:, None]
    )
    slot_index = row_owner * capacity + jnp.sum(same_owner.astype(jnp.int32), axis=1)
    dispatch = slot_index[:, None] == jnp.arange(slot_count, dtype=jnp.int32)[None, :]
    one_hot = dispatch.T

    def to_slots(rows_data):
        picked = jnp.tensordot(one_hot.astype(rows_data.dtype), rows_data, axes=1)
        return picked.reshape((peer_count, capacity) + rows_data.shape[1:])

    live_len = jnp.where(finished == 1, resp_len, 0).astype(jnp.bfloat16)
    own_all = jnp.concatenate([resp_cache, new_kv], axis=1)
    reply_iota = jnp.arange(resp_slots + step_count)
    pol_keys = policy_prompt[0, :, 0].reshape(prompt_width, kv_heads, HD)
    pol_values = policy_prompt[0, :, 1].reshape(prompt_width, kv_heads, HD)
    prompt_valid = jnp.arange(prompt_width) < prompt_len[0]
    resp_keys = own_all[:, :, 0].reshape(row_count, -1, kv_heads, HD)
    resp_values = own_all[:, :, 1].reshape(row_count, -1, kv_heads, HD)
    previous = jnp.zeros((row_count, q_width), jnp.float32)
    decoded_list = []
    query_list = []
    kept_list = []
    for step_idx in range(step_count):
        queries = (step_input[:, step_idx].astype(jnp.float32) + previous).astype(jnp.bfloat16)
        query_list.append(queries)
        received = lax.all_to_all(to_slots(queries), "dp", split_axis=0, concat_axis=0, tiled=True)
        lead_shape = received.shape[:2]
        prompt_queries = received.reshape(-1, kv_heads, group_size, HD)
        scores = (
            jnp.einsum(
                "skgd,tkd->skgt", prompt_queries, pol_keys, preferred_element_type=jnp.float32
            )
            * inv_scale
        )
        prompt_weight, prompt_weight_sum, prompt_top_score = softmax_pieces(scores, prompt_valid)
        prompt_summed = jnp.einsum(
            "skgt,tkd->skgd",
            prompt_weight.astype(jnp.bfloat16),
            pol_values,
            preferred_element_type=jnp.float32,
        )
        part_out = (
            (prompt_summed / prompt_weight_sum[..., None])
            .astype(jnp.bfloat16)
            .reshape(lead_shape + (q_width,))
        )
        part_lse = (prompt_top_score + jnp.log(prompt_weight_sum)).reshape(lead_shape + (q_heads,))
        back_out = lax.all_to_all(part_out, "dp", split_axis=0, concat_axis=0, tiled=True)
        back_lse = lax.all_to_all(part_lse, "dp", split_axis=0, concat_axis=0, tiled=True)
        results = (back_out, back_lse, received)
        back_out = results[0]
        back_lse = results[1]
        kept_list.append(results[2])
        prompt_out = jnp.dot(
            dispatch.astype(jnp.bfloat16),
            back_out.reshape(slot_count, q_width),
            preferred_element_type=jnp.float32,
        )
        prompt_lse = jnp.dot(
            dispatch.astype(jnp.float32),
            back_lse.reshape(slot_count, q_heads),
            precision=lax.Precision.HIGHEST,
        )
        query_heads = queries.reshape(row_count, kv_heads, group_size, HD)
        scores = (
            jnp.einsum(
                "rkgd,rtkd->rkgt", query_heads, resp_keys, preferred_element_type=jnp.float32
            )
            * inv_scale
        )
        reply_valid = jnp.where(
            reply_iota[None, :] < resp_slots,
            reply_iota[None, :] < resp_len[:, None],
            reply_iota[None, :] <= resp_slots + step_idx,
        )
        weight, weight_sum, top_score = softmax_pieces(scores, reply_valid[:, None, None, :])
        summed = jnp.einsum(
            "rkgt,rtkd->rkgd",
            weight.astype(jnp.bfloat16),
            resp_values,
            preferred_element_type=jnp.float32,
        )
        own_out = (summed / weight_sum[..., None]).reshape(row_count, q_heads, HD)
        own_lse = (top_score + jnp.log(weight_sum)).reshape(row_count, q_heads)
        joint_lse = jnp.maximum(prompt_lse, own_lse)
        prompt_wt = jnp.exp(prompt_lse - joint_lse)
        own_wt = jnp.exp(own_lse - joint_lse)
        blended = (
            prompt_wt[..., None] * prompt_out.reshape(row_count, q_heads, HD)
            + own_wt[..., None] * own_out
        ) / (prompt_wt + own_wt)[..., None]
        decoded_now = blended.reshape(row_count, q_width).astype(jnp.bfloat16)
        decoded_list.append(decoded_now)
        previous = lax.optimization_barrier(decoded_now).astype(jnp.float32)
    recv_kv, recv_live = (
        lax.all_to_all(to_slots(own_all), "dp", split_axis=0, concat_axis=0, tiled=True),
        lax.all_to_all(to_slots(live_len), "dp", split_axis=0, concat_axis=0, tiled=True),
    )
    recv_queries = jnp.stack(kept_list, axis=2)
    ref_keys = ref_prompt[0, :, 0].reshape(prompt_width, kv_heads, HD)
    ref_values = ref_prompt[0, :, 1].reshape(prompt_width, kv_heads, HD)
    slot_kv = recv_kv.reshape(slot_count, resp_slots + step_count, 2, kv_width)
    slot_keys = slot_kv[:, :, 0].reshape(slot_count, -1, kv_heads, HD)
    slot_values = slot_kv[:, :, 1].reshape(slot_count, -1, kv_heads, HD)
    slot_len = recv_live.reshape(slot_count).astype(jnp.int32)
    slot_queries = recv_queries.reshape(slot_count, step_count, q_width)
    probe_heads = probe.reshape(kv_heads, group_size, HD)
    prompt_mask = jnp.broadcast_to(prompt_valid[None, :], (slot_count, prompt_width))
    score_list = []
    for step_idx in range(step_count):
        queries = slot_queries[:, step_idx].reshape(slot_count, kv_heads, group_size, HD)
        prompt_scores = (
            jnp.einsum("skgd,tkd->skgt", queries, ref_keys, preferred_element_type=jnp.float32)
            * inv_scale
        )
        reply_scores = (
            jnp.einsum("skgd,stkd->skgt", queries, slot_keys, preferred_element_type=jnp.float32)
            * inv_scale
        )
        reply_valid = jnp.where(
            reply_iota[None, :] < resp_slots,
            reply_iota[None, :] < slot_len[:, None],
            reply_iota[None, :] <= resp_slots + step_idx,
        )
        key_valid = jnp.concatenate([prompt_mask, reply_valid], axis=1)
        weight, weight_sum, top_score = softmax_pieces(
            jnp.concatenate([prompt_scores, reply_scores], axis=-1), key_valid[:, None, None, :]
        )
        weight_low = weight.astype(jnp.bfloat16)
        summed = jnp.einsum(
            "skgt,tkd->skgd",
            weight_low[..., :prompt_width],
            ref_values,
            preferred_element_type=jnp.float32,
        )
        summed = summed + jnp.einsum(
            "skgt,stkd->skgd",
            weight_low[..., prompt_width:],
            slot_values,
            preferred_element_type=jnp.float32,
        )
        ref_out = summed / weight_sum[..., None]
        score_list.append(
            jnp.einsum("skgd,kgd->s", ref_out, probe_heads, precision=lax.Precision.HIGHEST)
        )
    head_terms = jnp.stack(score_list, axis=1)
    head_total = lax.psum(head_terms, "tensor")
    ref_score = jnp.where(slot_len[:, None] > 0, head_total, jnp.zeros((), jnp.float32)).reshape(
        1, slot_count, step_count
    )
    return (jnp.stack(decoded_list, axis=1), ref_score)


def dot_t(a, b):
    return lax.dot_general(a, b, (((1,), (1,)), ((), ())), preferred_element_type=jnp.float32)


def dot_n(a, b):
    return lax.dot_general(a, b, (((1,), (0,)), ((), ())), preferred_element_type=jnp.float32)


def softmax_part(z, valid, values):
    masked = jnp.where(valid, z, -jnp.inf)
    top = jnp.max(masked, axis=-1, keepdims=True)
    weight = jnp.exp2(masked - top)
    total = jnp.sum(weight, axis=-1, keepdims=True)
    acc = dot_n(weight.astype(jnp.bfloat16), values)
    return top, total, acc


def owner_block(dims, prompt, x_at, kv_at, lens, probe, put_decoded):
    rows, step_count, resp_slots, width, kv_heads, group = dims
    keys_n = resp_slots + step_count
    qrows = group * rows
    scale = LOG2E / math.sqrt(HD)
    prompt_valid = prompt(4)[0:1, :width].astype(jnp.float32) > 0.5
    len_q = jnp.concatenate([lens] * group, axis=0)
    q_iota = lax.broadcasted_iota(jnp.int32, (qrows, keys_n * rows), 0)
    k_iota = lax.broadcasted_iota(jnp.int32, (qrows, keys_n * rows), 1)
    same_row = lax.rem(q_iota, rows) == lax.rem(k_iota, rows)
    key_t = lax.div(k_iota, rows)
    cached = same_row & (key_t < resp_slots) & (key_t < len_q)
    fresh = same_row & (key_t >= resp_slots)
    own_keys, own_values = [], []
    for k in range(kv_heads):
        own_keys.append(
            jnp.concatenate([kv_at(t, 0, k) for t in range(keys_n)], axis=0).astype(jnp.bfloat16)
        )
        own_values.append(
            jnp.concatenate([kv_at(t, 1, k) for t in range(keys_n)], axis=0).astype(jnp.bfloat16)
        )
    previous = [None] * kv_heads
    scores = []
    for s in range(step_count):
        own_valid = cached | (fresh & (key_t <= resp_slots + s))
        score = jnp.zeros((rows, HD), jnp.float32)
        for k in range(kv_heads):
            cols = slice(k * HD, (k + 1) * HD)
            q = jnp.concatenate([x_at(s, k * group + g) for g in range(group)], axis=0)
            if s > 0:
                q = q + previous[k]
            q = q.astype(jnp.bfloat16)
            top_p, sum_p, acc_p = softmax_part(
                dot_t(q, prompt(0)[:, cols]) * scale, prompt_valid, prompt(1)[:, cols]
            )
            top_o, sum_o, acc_o = softmax_part(
                dot_t(q, own_keys[k]) * scale, own_valid, own_values[k]
            )
            prompt_out = (acc_p / sum_p).astype(jnp.bfloat16).astype(jnp.float32)
            joint = jnp.maximum(top_p, top_o)
            wt_p = sum_p * jnp.exp2(top_p - joint)
            ex_o = jnp.exp2(top_o - joint)
            inv = 1.0 / (wt_p + ex_o * sum_o)
            decoded = (wt_p * inv) * prompt_out + (ex_o * inv) * acc_o
            decoded = decoded.astype(jnp.bfloat16).astype(jnp.float32)
            previous[k] = decoded
            put_decoded(s, k, decoded)
            top_r, sum_r, acc_r = softmax_part(
                dot_t(q, prompt(2)[:, cols]) * scale, prompt_valid, prompt(3)[:, cols]
            )
            joint = jnp.maximum(top_r, top_o)
            ex_r = jnp.exp2(top_r - joint)
            ex_o = jnp.exp2(top_o - joint)
            inv = 1.0 / (ex_r * sum_r + ex_o * sum_o)
            ref_out = (ex_r * inv) * acc_r + (ex_o * inv) * acc_o
            for g in range(group):
                h = k * group + g
                score = score + ref_out[g * rows : (g + 1) * rows] * probe[h : h + 1]
        scores.append(jnp.sum(score, axis=-1, keepdims=True))
    lane = lax.broadcasted_iota(jnp.int32, (rows, HD), 1)
    out = jnp.zeros((rows, HD), jnp.float32)
    for s in range(step_count):
        out = jnp.where(lane == s, scores[s], out)
    return out


def compute_kernel(dims, blk_ref, x_ref, kv_ref, len_ref, probe_ref, dec_ref, score_ref):
    rows, step_count, resp_slots, width, kv_heads, group = dims

    def prompt(part):
        if part == 4:
            return blk_ref[0, 4 * width :, :]
        return blk_ref[0, part * width : (part + 1) * width, :]

    def x_at(s, h):
        return x_ref[s, :, h * HD : (h + 1) * HD]

    def kv_at(t, c, k):
        return kv_ref[t, c, :, k * HD : (k + 1) * HD]

    def put_decoded(s, k, decoded):
        for g in range(group):
            h = k * group + g
            dec_ref[s, :, h * HD : (h + 1) * HD] = decoded[g * rows : (g + 1) * rows]

    score_ref[...] = owner_block(
        dims, prompt, x_at, kv_at, len_ref[:, 0:1], probe_ref[...], put_decoded
    )


def per_device_gathered(
    step_input,
    new_kv,
    resp_cache,
    policy_prompt,
    ref_prompt,
    prompt_len,
    resp_len,
    row_owner,
    finished,
    probe,
):
    row_count, step_count, q_width = step_input.shape
    kv_width = new_kv.shape[3]
    q_heads = q_width // HD
    kv_heads = kv_width // HD
    group = q_heads // kv_heads
    peers = lax.axis_size("dp")
    capacity = max(2, (row_count + peers - 1) // peers)
    slots = peers * capacity
    resp_slots = resp_cache.shape[1]
    keys_n = resp_slots + step_count
    width = policy_prompt.shape[1]
    mask = (jnp.arange(kv_width) < prompt_len[0]).astype(jnp.bfloat16)
    block = jnp.concatenate(
        [
            policy_prompt[0, :, 0],
            policy_prompt[0, :, 1],
            ref_prompt[0, :, 0],
            ref_prompt[0, :, 1],
            jnp.broadcast_to(mask[None, :], (16, kv_width)),
        ],
        axis=0,
    )
    blocks = lax.all_gather(block, "dp")
    iota = jnp.arange(row_count, dtype=jnp.int32)
    earlier = (row_owner[:, None] == row_owner[None, :]) & (iota[None, :] < iota[:, None])
    slot_index = row_owner * capacity + jnp.sum(earlier.astype(jnp.int32), axis=1)
    place = slot_index[None, :] == jnp.arange(slots, dtype=jnp.int32)[:, None]
    one_hot = place.astype(jnp.bfloat16)
    x_slots = jnp.einsum("pr,rse->spe", one_hot, step_input, preferred_element_type=jnp.float32)
    own_all = jnp.concatenate([resp_cache, new_kv], axis=1)
    kv_slots = jnp.einsum("pr,rtce->tcpe", one_hot, own_all, preferred_element_type=jnp.float32)
    len_slots = jnp.sum(jnp.where(place, resp_len[None, :], 0), axis=1)
    done_slots = jnp.sum(jnp.where(place, finished[None, :], 0), axis=1)
    dims = (capacity, step_count, resp_slots, width, kv_heads, group)
    decoded, scores = pl.pallas_call(
        functools.partial(compute_kernel, dims),
        grid=(peers,),
        in_specs=[
            pl.BlockSpec((1, block.shape[0], kv_width), lambda o: (o, 0, 0)),
            pl.BlockSpec((step_count, capacity, q_width), lambda o: (0, o, 0)),
            pl.BlockSpec((keys_n, 2, capacity, kv_width), lambda o: (0, 0, o, 0)),
            pl.BlockSpec((capacity, HD), lambda o: (o, 0)),
            pl.BlockSpec((q_heads, HD), lambda o: (0, 0)),
        ],
        out_specs=[
            pl.BlockSpec((step_count, capacity, q_width), lambda o: (0, o, 0)),
            pl.BlockSpec((capacity, HD), lambda o: (o, 0)),
        ],
        out_shape=[
            jax.ShapeDtypeStruct((step_count, slots, q_width), jnp.float32),
            jax.ShapeDtypeStruct((slots, HD), jnp.float32),
        ],
        compiler_params=pltpu.CompilerParams(vmem_limit_bytes=40 * 1024 * 1024),
    )(
        blocks,
        x_slots,
        kv_slots,
        jnp.broadcast_to(len_slots[:, None], (slots, HD)),
        probe.reshape(q_heads, HD),
    )
    decoded_rows = jnp.einsum(
        "pr,spe->rse",
        one_hot,
        decoded.astype(jnp.bfloat16),
        preferred_element_type=jnp.float32,
    ).astype(jnp.bfloat16)
    scores = jnp.where(done_slots[:, None] == 1, scores[:, :step_count], 0.0)
    scores = scores.reshape(peers, capacity, step_count)
    received = lax.all_to_all(scores, "dp", split_axis=0, concat_axis=0, tiled=True)
    total = lax.psum(received, "tensor")
    return decoded_rows, total.reshape(1, slots, step_count)


def per_device(step_input, *rest):
    peers = lax.axis_size("dp")
    rows = step_input.shape[0]
    if rows % (8 * peers) == 0:
        return per_device_gathered(step_input, *rest)
    return per_device_routed(step_input, *rest)


def solution(mesh):
    in_specs = (
        P(("groups", "dp"), None, "tensor"),
        P(("groups", "dp"), None, None, "tensor"),
        P(("groups", "dp"), None, None, "tensor"),
        P(("groups", "dp"), None, None, "tensor"),
        P(("groups", "dp"), None, None, "tensor"),
        P(("groups", "dp")),
        P(("groups", "dp")),
        P(("groups", "dp")),
        P(("groups", "dp")),
        P("tensor"),
    )
    out_specs = (P(("groups", "dp"), None, "tensor"), P(("groups", "dp"), None, None))
    return jax.shard_map(
        per_device, mesh=mesh, in_specs=in_specs, out_specs=out_specs, check_vma=False
    )
```

```python
import functools
import math

import jax
import jax.numpy as jnp
from jax import lax
from jax.experimental import pallas as pl
from jax.experimental.pallas import tpu as pltpu
from jax.sharding import PartitionSpec as P

HD = 128
LOG2E = 1.4426950408889634


def softmax_pieces(scores, key_valid):
    masked = jnp.where(key_valid, scores, -jnp.inf)
    top_score = jnp.max(masked, axis=-1, keepdims=True)
    weight = jnp.exp(masked - top_score)
    return (weight, jnp.sum(weight, axis=-1), top_score[..., 0])


def per_device_routed(
    step_input,
    new_kv,
    resp_cache,
    policy_prompt,
    ref_prompt,
    prompt_len,
    resp_len,
    row_owner,
    finished,
    probe,
):
    row_count = step_input.shape[0]
    step_count = step_input.shape[1]
    q_width = step_input.shape[2]
    kv_width = new_kv.shape[3]
    q_heads = q_width // HD
    kv_heads = kv_width // HD
    group_size = q_heads // kv_heads
    inv_scale = 1.0 / math.sqrt(HD)
    peer_count = lax.axis_size("dp")
    capacity = max(2, (row_count + peer_count - 1) // peer_count)
    slot_count = peer_count * capacity
    resp_slots = resp_cache.shape[1]
    prompt_width = policy_prompt.shape[1]
    row_iota = jnp.arange(row_count, dtype=jnp.int32)
    same_owner = (row_owner[:, None] == row_owner[None, :]) & (
        row_iota[None, :] < row_iota[:, None]
    )
    slot_index = row_owner * capacity + jnp.sum(same_owner.astype(jnp.int32), axis=1)
    dispatch = slot_index[:, None] == jnp.arange(slot_count, dtype=jnp.int32)[None, :]
    one_hot = dispatch.T

    def to_slots(rows_data):
        picked = jnp.tensordot(one_hot.astype(rows_data.dtype), rows_data, axes=1)
        return picked.reshape((peer_count, capacity) + rows_data.shape[1:])

    live_len = jnp.where(finished == 1, resp_len, 0).astype(jnp.bfloat16)
    own_all = jnp.concatenate([resp_cache, new_kv], axis=1)
    reply_iota = jnp.arange(resp_slots + step_count)
    pol_keys = policy_prompt[0, :, 0].reshape(prompt_width, kv_heads, HD)
    pol_values = policy_prompt[0, :, 1].reshape(prompt_width, kv_heads, HD)
    prompt_valid = jnp.arange(prompt_width) < prompt_len[0]
    resp_keys = own_all[:, :, 0].reshape(row_count, -1, kv_heads, HD)
    resp_values = own_all[:, :, 1].reshape(row_count, -1, kv_heads, HD)
    previous = jnp.zeros((row_count, q_width), jnp.float32)
    decoded_list = []
    query_list = []
    kept_list = []
    for step_idx in range(step_count):
        queries = (step_input[:, step_idx].astype(jnp.float32) + previous).astype(jnp.bfloat16)
        query_list.append(queries)
        received = lax.all_to_all(to_slots(queries), "dp", split_axis=0, concat_axis=0, tiled=True)
        lead_shape = received.shape[:2]
        prompt_queries = received.reshape(-1, kv_heads, group_size, HD)
        scores = (
            jnp.einsum(
                "skgd,tkd->skgt", prompt_queries, pol_keys, preferred_element_type=jnp.float32
            )
            * inv_scale
        )
        prompt_weight, prompt_weight_sum, prompt_top_score = softmax_pieces(scores, prompt_valid)
        prompt_summed = jnp.einsum(
            "skgt,tkd->skgd",
            prompt_weight.astype(jnp.bfloat16),
            pol_values,
            preferred_element_type=jnp.float32,
        )
        part_out = (
            (prompt_summed / prompt_weight_sum[..., None])
            .astype(jnp.bfloat16)
            .reshape(lead_shape + (q_width,))
        )
        part_lse = (prompt_top_score + jnp.log(prompt_weight_sum)).reshape(lead_shape + (q_heads,))
        back_out = lax.all_to_all(part_out, "dp", split_axis=0, concat_axis=0, tiled=True)
        back_lse = lax.all_to_all(part_lse, "dp", split_axis=0, concat_axis=0, tiled=True)
        results = (back_out, back_lse, received)
        back_out = results[0]
        back_lse = results[1]
        kept_list.append(results[2])
        prompt_out = jnp.dot(
            dispatch.astype(jnp.bfloat16),
            back_out.reshape(slot_count, q_width),
            preferred_element_type=jnp.float32,
        )
        prompt_lse = jnp.dot(
            dispatch.astype(jnp.float32),
            back_lse.reshape(slot_count, q_heads),
            precision=lax.Precision.HIGHEST,
        )
        query_heads = queries.reshape(row_count, kv_heads, group_size, HD)
        scores = (
            jnp.einsum(
                "rkgd,rtkd->rkgt", query_heads, resp_keys, preferred_element_type=jnp.float32
            )
            * inv_scale
        )
        reply_valid = jnp.where(
            reply_iota[None, :] < resp_slots,
            reply_iota[None, :] < resp_len[:, None],
            reply_iota[None, :] <= resp_slots + step_idx,
        )
        weight, weight_sum, top_score = softmax_pieces(scores, reply_valid[:, None, None, :])
        summed = jnp.einsum(
            "rkgt,rtkd->rkgd",
            weight.astype(jnp.bfloat16),
            resp_values,
            preferred_element_type=jnp.float32,
        )
        own_out = (summed / weight_sum[..., None]).reshape(row_count, q_heads, HD)
        own_lse = (top_score + jnp.log(weight_sum)).reshape(row_count, q_heads)
        joint_lse = jnp.maximum(prompt_lse, own_lse)
        prompt_wt = jnp.exp(prompt_lse - joint_lse)
        own_wt = jnp.exp(own_lse - joint_lse)
        blended = (
            prompt_wt[..., None] * prompt_out.reshape(row_count, q_heads, HD)
            + own_wt[..., None] * own_out
        ) / (prompt_wt + own_wt)[..., None]
        decoded_now = blended.reshape(row_count, q_width).astype(jnp.bfloat16)
        decoded_list.append(decoded_now)
        previous = lax.optimization_barrier(decoded_now).astype(jnp.float32)
    recv_kv, recv_live = (
        lax.all_to_all(to_slots(own_all), "dp", split_axis=0, concat_axis=0, tiled=True),
        lax.all_to_all(to_slots(live_len), "dp", split_axis=0, concat_axis=0, tiled=True),
    )
    recv_queries = jnp.stack(kept_list, axis=2)
    ref_keys = ref_prompt[0, :, 0].reshape(prompt_width, kv_heads, HD)
    ref_values = ref_prompt[0, :, 1].reshape(prompt_width, kv_heads, HD)
    slot_kv = recv_kv.reshape(slot_count, resp_slots + step_count, 2, kv_width)
    slot_keys = slot_kv[:, :, 0].reshape(slot_count, -1, kv_heads, HD)
    slot_values = slot_kv[:, :, 1].reshape(slot_count, -1, kv_heads, HD)
    slot_len = recv_live.reshape(slot_count).astype(jnp.int32)
    slot_queries = recv_queries.reshape(slot_count, step_count, q_width)
    probe_heads = probe.reshape(kv_heads, group_size, HD)
    prompt_mask = jnp.broadcast_to(prompt_valid[None, :], (slot_count, prompt_width))
    score_list = []
    for step_idx in range(step_count):
        queries = slot_queries[:, step_idx].reshape(slot_count, kv_heads, group_size, HD)
        prompt_scores = (
            jnp.einsum("skgd,tkd->skgt", queries, ref_keys, preferred_element_type=jnp.float32)
            * inv_scale
        )
        reply_scores = (
            jnp.einsum("skgd,stkd->skgt", queries, slot_keys, preferred_element_type=jnp.float32)
            * inv_scale
        )
        reply_valid = jnp.where(
            reply_iota[None, :] < resp_slots,
            reply_iota[None, :] < slot_len[:, None],
            reply_iota[None, :] <= resp_slots + step_idx,
        )
        key_valid = jnp.concatenate([prompt_mask, reply_valid], axis=1)
        weight, weight_sum, top_score = softmax_pieces(
            jnp.concatenate([prompt_scores, reply_scores], axis=-1), key_valid[:, None, None, :]
        )
        weight_low = weight.astype(jnp.bfloat16)
        summed = jnp.einsum(
            "skgt,tkd->skgd",
            weight_low[..., :prompt_width],
            ref_values,
            preferred_element_type=jnp.float32,
        )
        summed = summed + jnp.einsum(
            "skgt,stkd->skgd",
            weight_low[..., prompt_width:],
            slot_values,
            preferred_element_type=jnp.float32,
        )
        ref_out = summed / weight_sum[..., None]
        score_list.append(
            jnp.einsum("skgd,kgd->s", ref_out, probe_heads, precision=lax.Precision.HIGHEST)
        )
    head_terms = jnp.stack(score_list, axis=1)
    head_total = lax.psum(head_terms, "tensor")
    ref_score = jnp.where(slot_len[:, None] > 0, head_total, jnp.zeros((), jnp.float32)).reshape(
        1, slot_count, step_count
    )
    return (jnp.stack(decoded_list, axis=1), ref_score)


def dot_n(a, b):
    return lax.dot_general(a, b, (((1,), (0,)), ((), ())), preferred_element_type=jnp.float32)


def softmax_part(z, valid, both_heads, values_t):
    masked = jnp.where(valid, z, -jnp.inf)
    top = jnp.max(masked, axis=0, keepdims=True)
    weight = jnp.exp2(masked - top)
    total = jnp.sum(weight, axis=0, keepdims=True)
    acc = dot_n(values_t, both_heads(weight.astype(jnp.bfloat16)))
    return top, total, acc


def owner_block(dims, prompt, prompt_len, x_at, kv_at, lens, probe_at, put_decoded, put_score):
    rows, step_count, resp_slots, width, kv_heads, group = dims
    keys_n = resp_slots + step_count
    padded = HD // rows
    lanes = 2 * group * rows
    pairs = kv_heads // 2
    scale = LOG2E / math.sqrt(HD)
    k_iota = lax.broadcasted_iota(jnp.int32, (HD, lanes), 0)
    q_iota = lax.broadcasted_iota(jnp.int32, (HD, lanes), 1)
    prompt_valid = k_iota.astype(jnp.float32) < prompt_len
    same_row = lax.rem(q_iota, rows) == lax.rem(k_iota, rows)
    key_t = lax.div(k_iota, rows)
    cached = same_row & (key_t < resp_slots) & (key_t < lens)
    fresh = same_row & (key_t >= resp_slots)
    first = (q_iota < lanes // 2).astype(jnp.float32)
    second = (1.0 - first).astype(jnp.bfloat16)
    first = first.astype(jnp.bfloat16)

    def both_heads(v):
        return jnp.concatenate([v * first, v * second], axis=0)

    blank = [jnp.zeros((rows, HD), jnp.float32)] * (padded - keys_n)

    def stacked(c, k):
        return jnp.concatenate([kv_at(t, c, k) for t in range(keys_n)] + blank, axis=0)

    keys, own_values = [], []
    for p in range(pairs):
        cols = slice(2 * p * HD, 2 * (p + 1) * HD)
        own = [stacked(0, 2 * p + i).astype(jnp.bfloat16) for i in range(2)]
        keys.append(
            jnp.concatenate(
                [prompt(0)[:, cols], prompt(2)[:, cols], jnp.concatenate(own, axis=1)], axis=0
            )
        )
        own = [stacked(1, 2 * p + i).T.astype(jnp.bfloat16) for i in range(2)]
        own_values.append(jnp.concatenate(own, axis=1))
    previous = [None] * pairs
    for s in range(step_count):
        own_valid = cached | (fresh & (key_t <= resp_slots + s))
        score = None
        for p in range(pairs):
            cols = slice(2 * p * HD, 2 * (p + 1) * HD)
            heads = range(2 * p * group, 2 * (p + 1) * group)
            q = jnp.concatenate([x_at(s, h) for h in heads], axis=0).T
            if s > 0:
                q = q + previous[p]
            z = dot_n(keys[p], both_heads(q.astype(jnp.bfloat16))) * scale
            top_p, sum_p, acc_p = softmax_part(
                z[:width], prompt_valid, both_heads, prompt(1)[:, cols]
            )
            top_o, sum_o, acc_o = softmax_part(
                z[2 * width :], own_valid, both_heads, own_values[p]
            )
            prompt_out = (acc_p * (1.0 / sum_p)).astype(jnp.bfloat16).astype(jnp.float32)
            joint = jnp.maximum(top_p, top_o)
            wt_p = sum_p * jnp.exp2(top_p - joint)
            ex_o = jnp.exp2(top_o - joint)
            inv = 1.0 / (wt_p + ex_o * sum_o)
            decoded = (wt_p * inv) * prompt_out + (ex_o * inv) * acc_o
            decoded = decoded.astype(jnp.bfloat16).astype(jnp.float32)
            previous[p] = decoded
            put_decoded(s, p, decoded.T)
            top_r, sum_r, acc_r = softmax_part(
                z[width : 2 * width], prompt_valid, both_heads, prompt(3)[:, cols]
            )
            joint = jnp.maximum(top_r, top_o)
            ex_r = jnp.exp2(top_r - joint)
            ex_o = jnp.exp2(top_o - joint)
            inv = 1.0 / (ex_r * sum_r + ex_o * sum_o)
            probe = probe_at(p)
            term = (ex_r * inv) * jnp.sum(acc_r * probe, axis=0, keepdims=True)
            term = term + (ex_o * inv) * jnp.sum(acc_o * probe, axis=0, keepdims=True)
            score = term if score is None else score + term
        put_score(s, score)


def compute_kernel(dims, blk_ref, x_ref, kv_ref, len_ref, probe_ref, dec_ref, score_ref):
    rows, step_count, resp_slots, width, kv_heads, group = dims

    def prompt(part):
        return blk_ref[0, part * width : (part + 1) * width, :]

    def x_at(s, h):
        return x_ref[s, :, h * HD : (h + 1) * HD]

    def kv_at(t, c, k):
        return kv_ref[t, c, :, k * HD : (k + 1) * HD]

    def put_decoded(s, p, decoded):
        for i in range(2 * group):
            h = 2 * p * group + i
            dec_ref[s, :, h * HD : (h + 1) * HD] = decoded[i * rows : (i + 1) * rows]

    def put_score(s, score):
        score_ref[0, s : s + 1, :] = score

    prompt_len = blk_ref[0, 4 * width :, :HD][0:1].astype(jnp.float32)
    owner_block(
        dims,
        prompt,
        prompt_len,
        x_at,
        kv_at,
        len_ref[0, 0:1, :],
        lambda p: probe_ref[p],
        put_decoded,
        put_score,
    )


def per_device_gathered(
    step_input,
    new_kv,
    resp_cache,
    policy_prompt,
    ref_prompt,
    prompt_len,
    resp_len,
    row_owner,
    finished,
    probe,
):
    row_count, step_count, q_width = step_input.shape
    kv_width = new_kv.shape[3]
    q_heads = q_width // HD
    kv_heads = kv_width // HD
    group = q_heads // kv_heads
    peers = lax.axis_size("dp")
    capacity = max(2, (row_count + peers - 1) // peers)
    slots = peers * capacity
    resp_slots = resp_cache.shape[1]
    keys_n = resp_slots + step_count
    width = policy_prompt.shape[1]
    lanes = 2 * group * capacity
    pairs = kv_heads // 2

    def turned(values):
        by_head = values.reshape(width, kv_heads, HD)
        return jnp.transpose(by_head, (2, 1, 0)).reshape(HD, kv_heads * width)

    block = jnp.concatenate(
        [
            policy_prompt[0, :, 0],
            turned(policy_prompt[0, :, 1]),
            ref_prompt[0, :, 0],
            turned(ref_prompt[0, :, 1]),
            jnp.broadcast_to(prompt_len.astype(jnp.bfloat16)[None, :], (16, kv_width)),
        ],
        axis=0,
    )
    blocks = lax.all_gather(block, "dp")
    iota = jnp.arange(row_count, dtype=jnp.int32)
    earlier = (row_owner[:, None] == row_owner[None, :]) & (iota[None, :] < iota[:, None])
    slot_index = row_owner * capacity + jnp.sum(earlier.astype(jnp.int32), axis=1)
    place = slot_index[None, :] == jnp.arange(slots, dtype=jnp.int32)[:, None]
    one_hot = place.astype(jnp.bfloat16)
    x_slots = jnp.einsum("pr,rse->spe", one_hot, step_input, preferred_element_type=jnp.float32)
    own_all = jnp.concatenate([resp_cache, new_kv], axis=1)
    kv_slots = jnp.einsum("pr,rtce->tcpe", one_hot, own_all, preferred_element_type=jnp.float32)
    len_slots = jnp.sum(jnp.where(place, resp_len[None, :], 0), axis=1)
    done_slots = jnp.sum(jnp.where(place, finished[None, :], 0), axis=1)
    dims = (capacity, step_count, resp_slots, width, kv_heads, group)
    decoded, scores = pl.pallas_call(
        functools.partial(compute_kernel, dims),
        grid=(peers,),
        in_specs=[
            pl.BlockSpec((1, block.shape[0], kv_width), lambda o: (o, 0, 0)),
            pl.BlockSpec((step_count, capacity, q_width), lambda o: (0, o, 0)),
            pl.BlockSpec((keys_n, 2, capacity, kv_width), lambda o: (0, 0, o, 0)),
            pl.BlockSpec((1, 8, lanes), lambda o: (o, 0, 0)),
            pl.BlockSpec((pairs, HD, lanes), lambda o: (0, 0, 0)),
        ],
        out_specs=[
            pl.BlockSpec((step_count, capacity, q_width), lambda o: (0, o, 0)),
            pl.BlockSpec((1, step_count, lanes), lambda o: (o, 0, 0)),
        ],
        out_shape=[
            jax.ShapeDtypeStruct((step_count, slots, q_width), jnp.float32),
            jax.ShapeDtypeStruct((peers, step_count, lanes), jnp.float32),
        ],
        compiler_params=pltpu.CompilerParams(vmem_limit_bytes=40 * 1024 * 1024),
    )(
        blocks,
        x_slots,
        kv_slots,
        jnp.broadcast_to(
            len_slots.reshape(peers, 1, 1, capacity), (peers, 8, 2 * group, capacity)
        ).reshape(peers, 8, lanes),
        jnp.repeat(
            jnp.transpose(probe.reshape(pairs, 2 * group, HD), (0, 2, 1)), capacity, axis=2
        ),
    )
    decoded_rows = jnp.einsum(
        "pr,spe->rse",
        one_hot,
        decoded.astype(jnp.bfloat16),
        preferred_element_type=jnp.float32,
    ).astype(jnp.bfloat16)
    scores = scores.reshape(peers, step_count, 2 * group, capacity)
    scores = jnp.transpose(jnp.sum(scores, axis=2), (0, 2, 1))
    scores = jnp.where(done_slots.reshape(peers, capacity, 1) == 1, scores, 0.0)
    received = lax.all_to_all(scores, "dp", split_axis=0, concat_axis=0, tiled=True)
    total = lax.psum(received, "tensor")
    return decoded_rows, total.reshape(1, slots, step_count)


def per_device(step_input, *rest):
    peers = lax.axis_size("dp")
    rows = step_input.shape[0]
    step_count, q_width = step_input.shape[1:]
    resp_slots, kv_width = rest[1].shape[1], rest[1].shape[3]
    fits = (
        rows == 8 * peers
        and rest[2].shape[1] == HD
        and 16 * q_width == HD * kv_width
        and kv_width % (2 * HD) == 0
        and 8 * (resp_slots + step_count) <= HD
    )
    if fits:
        return per_device_gathered(step_input, *rest)
    return per_device_routed(step_input, *rest)


def solution(mesh):
    in_specs = (
        P(("groups", "dp"), None, "tensor"),
        P(("groups", "dp"), None, None, "tensor"),
        P(("groups", "dp"), None, None, "tensor"),
        P(("groups", "dp"), None, None, "tensor"),
        P(("groups", "dp"), None, None, "tensor"),
        P(("groups", "dp")),
        P(("groups", "dp")),
        P(("groups", "dp")),
        P(("groups", "dp")),
        P("tensor"),
    )
    out_specs = (P(("groups", "dp"), None, "tensor"), P(("groups", "dp"), None, None))
    return jax.shard_map(
        per_device, mesh=mesh, in_specs=in_specs, out_specs=out_specs, check_vma=False
    )
```

```python
import functools
import math

import jax
import jax.numpy as jnp
from jax import lax
from jax.experimental import pallas as pl
from jax.experimental.pallas import tpu as pltpu
from jax.sharding import PartitionSpec as P

HD = 128
LOG2E = 1.4426950408889634


def softmax_pieces(scores, key_valid):
    masked = jnp.where(key_valid, scores, -jnp.inf)
    top_score = jnp.max(masked, axis=-1, keepdims=True)
    weight = jnp.exp(masked - top_score)
    return (weight, jnp.sum(weight, axis=-1), top_score[..., 0])


def per_device_routed(
    step_input,
    new_kv,
    resp_cache,
    policy_prompt,
    ref_prompt,
    prompt_len,
    resp_len,
    row_owner,
    finished,
    probe,
):
    row_count = step_input.shape[0]
    step_count = step_input.shape[1]
    q_width = step_input.shape[2]
    kv_width = new_kv.shape[3]
    q_heads = q_width // HD
    kv_heads = kv_width // HD
    group_size = q_heads // kv_heads
    inv_scale = 1.0 / math.sqrt(HD)
    peer_count = lax.axis_size("dp")
    capacity = max(2, (row_count + peer_count - 1) // peer_count)
    slot_count = peer_count * capacity
    resp_slots = resp_cache.shape[1]
    prompt_width = policy_prompt.shape[1]
    row_iota = jnp.arange(row_count, dtype=jnp.int32)
    same_owner = (row_owner[:, None] == row_owner[None, :]) & (
        row_iota[None, :] < row_iota[:, None]
    )
    slot_index = row_owner * capacity + jnp.sum(same_owner.astype(jnp.int32), axis=1)
    dispatch = slot_index[:, None] == jnp.arange(slot_count, dtype=jnp.int32)[None, :]
    one_hot = dispatch.T

    def to_slots(rows_data):
        picked = jnp.tensordot(one_hot.astype(rows_data.dtype), rows_data, axes=1)
        return picked.reshape((peer_count, capacity) + rows_data.shape[1:])

    live_len = jnp.where(finished == 1, resp_len, 0).astype(jnp.bfloat16)
    own_all = jnp.concatenate([resp_cache, new_kv], axis=1)
    reply_iota = jnp.arange(resp_slots + step_count)
    pol_keys = policy_prompt[0, :, 0].reshape(prompt_width, kv_heads, HD)
    pol_values = policy_prompt[0, :, 1].reshape(prompt_width, kv_heads, HD)
    prompt_valid = jnp.arange(prompt_width) < prompt_len[0]
    resp_keys = own_all[:, :, 0].reshape(row_count, -1, kv_heads, HD)
    resp_values = own_all[:, :, 1].reshape(row_count, -1, kv_heads, HD)
    previous = jnp.zeros((row_count, q_width), jnp.float32)
    decoded_list = []
    query_list = []
    kept_list = []
    for step_idx in range(step_count):
        queries = (step_input[:, step_idx].astype(jnp.float32) + previous).astype(jnp.bfloat16)
        query_list.append(queries)
        received = lax.all_to_all(to_slots(queries), "dp", split_axis=0, concat_axis=0, tiled=True)
        lead_shape = received.shape[:2]
        prompt_queries = received.reshape(-1, kv_heads, group_size, HD)
        scores = (
            jnp.einsum(
                "skgd,tkd->skgt", prompt_queries, pol_keys, preferred_element_type=jnp.float32
            )
            * inv_scale
        )
        prompt_weight, prompt_weight_sum, prompt_top_score = softmax_pieces(scores, prompt_valid)
        prompt_summed = jnp.einsum(
            "skgt,tkd->skgd",
            prompt_weight.astype(jnp.bfloat16),
            pol_values,
            preferred_element_type=jnp.float32,
        )
        part_out = (
            (prompt_summed / prompt_weight_sum[..., None])
            .astype(jnp.bfloat16)
            .reshape(lead_shape + (q_width,))
        )
        part_lse = (prompt_top_score + jnp.log(prompt_weight_sum)).reshape(lead_shape + (q_heads,))
        back_out = lax.all_to_all(part_out, "dp", split_axis=0, concat_axis=0, tiled=True)
        back_lse = lax.all_to_all(part_lse, "dp", split_axis=0, concat_axis=0, tiled=True)
        results = (back_out, back_lse, received)
        back_out = results[0]
        back_lse = results[1]
        kept_list.append(results[2])
        prompt_out = jnp.dot(
            dispatch.astype(jnp.bfloat16),
            back_out.reshape(slot_count, q_width),
            preferred_element_type=jnp.float32,
        )
        prompt_lse = jnp.dot(
            dispatch.astype(jnp.float32),
            back_lse.reshape(slot_count, q_heads),
            precision=lax.Precision.HIGHEST,
        )
        query_heads = queries.reshape(row_count, kv_heads, group_size, HD)
        scores = (
            jnp.einsum(
                "rkgd,rtkd->rkgt", query_heads, resp_keys, preferred_element_type=jnp.float32
            )
            * inv_scale
        )
        reply_valid = jnp.where(
            reply_iota[None, :] < resp_slots,
            reply_iota[None, :] < resp_len[:, None],
            reply_iota[None, :] <= resp_slots + step_idx,
        )
        weight, weight_sum, top_score = softmax_pieces(scores, reply_valid[:, None, None, :])
        summed = jnp.einsum(
            "rkgt,rtkd->rkgd",
            weight.astype(jnp.bfloat16),
            resp_values,
            preferred_element_type=jnp.float32,
        )
        own_out = (summed / weight_sum[..., None]).reshape(row_count, q_heads, HD)
        own_lse = (top_score + jnp.log(weight_sum)).reshape(row_count, q_heads)
        joint_lse = jnp.maximum(prompt_lse, own_lse)
        prompt_wt = jnp.exp(prompt_lse - joint_lse)
        own_wt = jnp.exp(own_lse - joint_lse)
        blended = (
            prompt_wt[..., None] * prompt_out.reshape(row_count, q_heads, HD)
            + own_wt[..., None] * own_out
        ) / (prompt_wt + own_wt)[..., None]
        decoded_now = blended.reshape(row_count, q_width).astype(jnp.bfloat16)
        decoded_list.append(decoded_now)
        previous = lax.optimization_barrier(decoded_now).astype(jnp.float32)
    recv_kv, recv_live = (
        lax.all_to_all(to_slots(own_all), "dp", split_axis=0, concat_axis=0, tiled=True),
        lax.all_to_all(to_slots(live_len), "dp", split_axis=0, concat_axis=0, tiled=True),
    )
    recv_queries = jnp.stack(kept_list, axis=2)
    ref_keys = ref_prompt[0, :, 0].reshape(prompt_width, kv_heads, HD)
    ref_values = ref_prompt[0, :, 1].reshape(prompt_width, kv_heads, HD)
    slot_kv = recv_kv.reshape(slot_count, resp_slots + step_count, 2, kv_width)
    slot_keys = slot_kv[:, :, 0].reshape(slot_count, -1, kv_heads, HD)
    slot_values = slot_kv[:, :, 1].reshape(slot_count, -1, kv_heads, HD)
    slot_len = recv_live.reshape(slot_count).astype(jnp.int32)
    slot_queries = recv_queries.reshape(slot_count, step_count, q_width)
    probe_heads = probe.reshape(kv_heads, group_size, HD)
    prompt_mask = jnp.broadcast_to(prompt_valid[None, :], (slot_count, prompt_width))
    score_list = []
    for step_idx in range(step_count):
        queries = slot_queries[:, step_idx].reshape(slot_count, kv_heads, group_size, HD)
        prompt_scores = (
            jnp.einsum("skgd,tkd->skgt", queries, ref_keys, preferred_element_type=jnp.float32)
            * inv_scale
        )
        reply_scores = (
            jnp.einsum("skgd,stkd->skgt", queries, slot_keys, preferred_element_type=jnp.float32)
            * inv_scale
        )
        reply_valid = jnp.where(
            reply_iota[None, :] < resp_slots,
            reply_iota[None, :] < slot_len[:, None],
            reply_iota[None, :] <= resp_slots + step_idx,
        )
        key_valid = jnp.concatenate([prompt_mask, reply_valid], axis=1)
        weight, weight_sum, top_score = softmax_pieces(
            jnp.concatenate([prompt_scores, reply_scores], axis=-1), key_valid[:, None, None, :]
        )
        weight_low = weight.astype(jnp.bfloat16)
        summed = jnp.einsum(
            "skgt,tkd->skgd",
            weight_low[..., :prompt_width],
            ref_values,
            preferred_element_type=jnp.float32,
        )
        summed = summed + jnp.einsum(
            "skgt,stkd->skgd",
            weight_low[..., prompt_width:],
            slot_values,
            preferred_element_type=jnp.float32,
        )
        ref_out = summed / weight_sum[..., None]
        score_list.append(
            jnp.einsum("skgd,kgd->s", ref_out, probe_heads, precision=lax.Precision.HIGHEST)
        )
    head_terms = jnp.stack(score_list, axis=1)
    head_total = lax.psum(head_terms, "tensor")
    ref_score = jnp.where(slot_len[:, None] > 0, head_total, jnp.zeros((), jnp.float32)).reshape(
        1, slot_count, step_count
    )
    return (jnp.stack(decoded_list, axis=1), ref_score)


def dot_n(a, b):
    return lax.dot_general(a, b, (((1,), (0,)), ((), ())), preferred_element_type=jnp.float32)


def softmax_part(z, valid, both_heads, values_t):
    masked = jnp.where(valid, z, -jnp.inf)
    top = jnp.max(masked, axis=0, keepdims=True)
    weight = jnp.exp2(masked - top)
    total = jnp.sum(weight, axis=0, keepdims=True)
    acc = dot_n(values_t, both_heads(weight.astype(jnp.bfloat16)))
    return top, total, acc


def owner_block(dims, prompt, prompt_len, x_at, kv_at, lens, probe_at, put_decoded, put_score):
    rows, step_count, resp_slots, width, kv_heads, group = dims
    keys_n = resp_slots + step_count
    padded = HD // rows
    lanes = 2 * group * rows
    pairs = kv_heads // 2
    scale = LOG2E / math.sqrt(HD)
    k_iota = lax.broadcasted_iota(jnp.int32, (HD, lanes), 0)
    q_iota = lax.broadcasted_iota(jnp.int32, (HD, lanes), 1)
    prompt_valid = k_iota.astype(jnp.float32) < prompt_len
    same_row = lax.rem(q_iota, rows) == lax.rem(k_iota, rows)
    key_t = lax.div(k_iota, rows)
    cached = same_row & (key_t < resp_slots) & (key_t < lens)
    fresh = same_row & (key_t >= resp_slots)
    first = (q_iota < lanes // 2).astype(jnp.float32)
    second = (1.0 - first).astype(jnp.bfloat16)
    first = first.astype(jnp.bfloat16)

    def both_heads(v):
        return jnp.concatenate([v * first, v * second], axis=0)

    blank = [jnp.zeros((rows, HD), jnp.float32)] * (padded - keys_n)

    def stacked(c, k):
        return jnp.concatenate([kv_at(t, c, k) for t in range(keys_n)] + blank, axis=0)

    keys, own_values = [], []
    for p in range(pairs):
        cols = slice(2 * p * HD, 2 * (p + 1) * HD)
        own = [stacked(0, 2 * p + i).astype(jnp.bfloat16) for i in range(2)]
        keys.append(
            jnp.concatenate(
                [prompt(0)[:, cols], prompt(2)[:, cols], jnp.concatenate(own, axis=1)], axis=0
            )
        )
        own = [stacked(1, 2 * p + i).T.astype(jnp.bfloat16) for i in range(2)]
        own_values.append(jnp.concatenate(own, axis=1))
    previous = [None] * pairs
    for s in range(step_count):
        own_valid = cached | (fresh & (key_t <= resp_slots + s))
        score = None
        for p in range(pairs):
            cols = slice(2 * p * HD, 2 * (p + 1) * HD)
            heads = range(2 * p * group, 2 * (p + 1) * group)
            q = jnp.concatenate([x_at(s, h) for h in heads], axis=0).T
            if s > 0:
                q = q + previous[p]
            z = dot_n(keys[p], both_heads(q.astype(jnp.bfloat16))) * scale
            top_p, sum_p, acc_p = softmax_part(
                z[:width], prompt_valid, both_heads, prompt(1)[:, cols]
            )
            top_o, sum_o, acc_o = softmax_part(
                z[2 * width :], own_valid, both_heads, own_values[p]
            )
            prompt_out = (acc_p * (1.0 / sum_p)).astype(jnp.bfloat16).astype(jnp.float32)
            joint = jnp.maximum(top_p, top_o)
            wt_p = sum_p * jnp.exp2(top_p - joint)
            ex_o = jnp.exp2(top_o - joint)
            inv = 1.0 / (wt_p + ex_o * sum_o)
            decoded = (wt_p * inv) * prompt_out + (ex_o * inv) * acc_o
            decoded = decoded.astype(jnp.bfloat16).astype(jnp.float32)
            previous[p] = decoded
            put_decoded(s, p, decoded.T)
            top_r, sum_r, acc_r = softmax_part(
                z[width : 2 * width], prompt_valid, both_heads, prompt(3)[:, cols]
            )
            joint = jnp.maximum(top_r, top_o)
            ex_r = jnp.exp2(top_r - joint)
            ex_o = jnp.exp2(top_o - joint)
            inv = 1.0 / (ex_r * sum_r + ex_o * sum_o)
            probe = probe_at(p)
            term = (ex_r * inv) * jnp.sum(acc_r * probe, axis=0, keepdims=True)
            term = term + (ex_o * inv) * jnp.sum(acc_o * probe, axis=0, keepdims=True)
            score = term if score is None else score + term
        put_score(s, score)


def fused_kernel(
    dims,
    blk_ref,
    x_ref,
    kv_ref,
    len_ref,
    done_ref,
    probe_ref,
    dec_ref,
    score_ref,
    buf,
    mail,
    got,
    own_sem,
    send_sem,
    recv_sem,
    mail_send,
    mail_recv,
):
    rows, step_count, resp_slots, width, kv_heads, group = dims
    n = buf.shape[0]
    half = n // 2
    tensors = got.shape[0]
    part = lax.axis_index("groups")
    me = lax.axis_index("dp")
    tau = lax.axis_index("tensor")
    z = lax.div(me, 2)
    y = lax.rem(me, 2)

    def device(dp, t):
        return (part, dp, t)

    barrier = pltpu.get_barrier_semaphore()
    for dt in range(tensors):
        for j in range(n):
            if dt or j:
                pl.semaphore_signal(
                    barrier,
                    inc=1,
                    device_id=device(lax.rem(me + j, n), lax.rem(tau + dt, tensors)),
                    device_id_type=pl.DeviceIdType.MESH,
                )
    pl.semaphore_wait(barrier, tensors * n - 1)

    across = me + 1 - 2 * y
    targets = (jnp.minimum(me + 2, n - 2 + y), jnp.maximum(me - 2, y), across)

    def hop(src, o, way):
        return pltpu.make_async_remote_copy(
            src_ref=src,
            dst_ref=buf.at[o],
            send_sem=send_sem.at[way, o],
            recv_sem=recv_sem.at[o],
            device_id=device(targets[way], tau),
            device_id_type=pl.DeviceIdType.MESH,
        )

    def each_way(zz, act):
        o = 2 * zz + y
        pl.when((z < half - 1) & (zz <= z))(lambda: act(o, 0))
        pl.when((z > 0) & (zz >= z))(lambda: act(o, 1))
        act(o, 2)

    each_way(z, lambda o, way: hop(blk_ref, o, way).start())
    own = pltpu.make_async_copy(blk_ref, buf.at[me], own_sem)
    own.start()
    own.wait()

    def by_distance(i):
        up, down = half - 1 - z, z
        near = jnp.minimum(up, down)
        paired = lax.div(i + 1, 2) * jnp.where(lax.rem(i, 2) == 1, 1, -1)
        beyond = (i - near) * jnp.where(up > down, 1, -1)
        return z + jnp.where(i <= 2 * near, paired, beyond)

    def letter(o, dt):
        return pltpu.make_async_remote_copy(
            src_ref=mail.at[o],
            dst_ref=got.at[tau, me],
            send_sem=mail_send.at[dt, o],
            recv_sem=mail_recv.at[tau, me],
            device_id=device(o, lax.rem(tau + dt, tensors)),
            device_id_type=pl.DeviceIdType.MESH,
        )

    def turn(t, carry):
        odd = lax.rem(t, 2) == 1
        last = t == n - 1
        line = (t == 0) | (odd & jnp.logical_not(last))
        order = jnp.where(
            line, lax.div(t + 1, 2), jnp.where(last, half - 1, lax.div(t, 2) - 1)
        )
        zz = by_distance(order)
        o = 2 * zz + jnp.where(line, y, 1 - y)

        @pl.when(t > 0)
        def _():
            hop(buf.at[o], o, 2).wait_recv()

        @pl.when((t > 0) & line)
        def _():
            each_way(zz, lambda b, way: hop(buf.at[b], b, way).start())

        here = pl.ds(pl.multiple_of(o * rows, rows), rows)

        def put_decoded(s, p, decoded):
            for i in range(2 * group):
                h = 2 * p * group + i
                dec_ref[s, here, h * HD : (h + 1) * HD] = decoded[i * rows : (i + 1) * rows]

        def put_score(s, score):
            mail[o, s : s + 1, :] = jnp.where(done_ref[o, 0:1, :] == 1, score, 0.0)

        owner_block(
            dims,
            lambda i: buf[o, i * width : (i + 1) * width, :],
            buf[o, 4 * width :, :HD][0:1].astype(jnp.float32),
            lambda s, h: x_ref[s, here, h * HD : (h + 1) * HD],
            lambda t, c, k: kv_ref[t, c, here, k * HD : (k + 1) * HD],
            len_ref[o, 0:1, :],
            lambda p: probe_ref[p],
            put_decoded,
            put_score,
        )
        for dt in range(1, tensors):
            letter(o, dt).start()
        pl.when(o != me)(lambda: letter(o, 0).start())

        @pl.when(o == me)
        def _():
            got[tau, me] = mail[me]

        return carry

    mail[...] = jnp.zeros_like(mail)
    lax.fori_loop(0, n, turn, 0)

    def arrived(t, b):
        return pltpu.make_async_remote_copy(
            src_ref=mail.at[b],
            dst_ref=got.at[t, b],
            send_sem=mail_send.at[0, b],
            recv_sem=mail_recv.at[t, b],
            device_id=device(across, tau),
            device_id_type=pl.DeviceIdType.MESH,
        )

    def finish(b, carry):
        for dt in range(1, tensors):
            arrived(lax.rem(tau + dt, tensors), b).wait_recv()
            letter(b, dt).wait_send()

        @pl.when(b != me)
        def _():
            arrived(tau, b).wait_recv()
            letter(b, 0).wait_send()

        return carry

    lax.fori_loop(0, n, finish, 0)

    def sent(zz, carry):
        each_way(zz, lambda o, way: hop(buf.at[o], o, way).wait_send())
        return carry

    lax.fori_loop(0, half, sent, 0)
    total = got[0]
    for t in range(1, tensors):
        total = total + got[t]
    score_ref[...] = total


def per_device_gathered(
    step_input,
    new_kv,
    resp_cache,
    policy_prompt,
    ref_prompt,
    prompt_len,
    resp_len,
    row_owner,
    finished,
    probe,
):
    row_count, step_count, q_width = step_input.shape
    kv_width = new_kv.shape[3]
    q_heads = q_width // HD
    kv_heads = kv_width // HD
    group = q_heads // kv_heads
    peers = lax.axis_size("dp")
    capacity = max(2, (row_count + peers - 1) // peers)
    slots = peers * capacity
    resp_slots = resp_cache.shape[1]
    keys_n = resp_slots + step_count
    width = policy_prompt.shape[1]
    lanes = 2 * group * capacity
    pairs = kv_heads // 2

    def turned(values):
        by_head = values.reshape(width, kv_heads, HD)
        return jnp.transpose(by_head, (2, 1, 0)).reshape(HD, kv_heads * width)

    block = jnp.concatenate(
        [
            policy_prompt[0, :, 0],
            turned(policy_prompt[0, :, 1]),
            ref_prompt[0, :, 0],
            turned(ref_prompt[0, :, 1]),
            jnp.broadcast_to(prompt_len.astype(jnp.bfloat16)[None, :], (16, kv_width)),
        ],
        axis=0,
    )
    iota = jnp.arange(row_count, dtype=jnp.int32)
    earlier = (row_owner[:, None] == row_owner[None, :]) & (iota[None, :] < iota[:, None])
    slot_index = row_owner * capacity + jnp.sum(earlier.astype(jnp.int32), axis=1)
    place = slot_index[None, :] == jnp.arange(slots, dtype=jnp.int32)[:, None]
    one_hot = place.astype(jnp.bfloat16)
    x_slots = jnp.einsum("pr,rse->spe", one_hot, step_input, preferred_element_type=jnp.float32)
    own_all = jnp.concatenate([resp_cache, new_kv], axis=1)
    kv_slots = jnp.einsum("pr,rtce->tcpe", one_hot, own_all, preferred_element_type=jnp.float32)
    len_slots = jnp.sum(jnp.where(place, resp_len[None, :], 0), axis=1)
    done_slots = jnp.sum(jnp.where(place, finished[None, :], 0), axis=1)
    dims = (capacity, step_count, resp_slots, width, kv_heads, group)

    def on_lanes(values):
        by_slot = values.reshape(peers, 1, 1, capacity)
        return jnp.broadcast_to(by_slot, (peers, 8, 2 * group, capacity)).reshape(
            peers, 8, lanes
        )

    tensors = lax.axis_size("tensor")
    vmem = pl.BlockSpec(memory_space=pltpu.VMEM)
    decoded, scores = pl.pallas_call(
        functools.partial(fused_kernel, dims),
        in_specs=[vmem] * 6,
        out_specs=[vmem] * 2,
        out_shape=[
            jax.ShapeDtypeStruct((step_count, slots, q_width), jnp.float32),
            jax.ShapeDtypeStruct((peers, 8, lanes), jnp.float32),
        ],
        scratch_shapes=[
            pltpu.VMEM((peers,) + block.shape, jnp.bfloat16),
            pltpu.VMEM((peers, 8, lanes), jnp.float32),
            pltpu.VMEM((tensors, peers, 8, lanes), jnp.float32),
            pltpu.SemaphoreType.DMA,
            pltpu.SemaphoreType.DMA((3, peers)),
            pltpu.SemaphoreType.DMA((peers,)),
            pltpu.SemaphoreType.DMA((tensors, peers)),
            pltpu.SemaphoreType.DMA((tensors, peers)),
        ],
        compiler_params=pltpu.CompilerParams(
            collective_id=0, has_side_effects=True, vmem_limit_bytes=48 * 1024 * 1024
        ),
    )(
        block,
        x_slots,
        kv_slots,
        on_lanes(len_slots),
        on_lanes(done_slots),
        jnp.repeat(
            jnp.transpose(probe.reshape(pairs, 2 * group, HD), (0, 2, 1)), capacity, axis=2
        ),
    )
    decoded_rows = jnp.einsum(
        "pr,spe->rse",
        one_hot,
        decoded.astype(jnp.bfloat16),
        preferred_element_type=jnp.float32,
    ).astype(jnp.bfloat16)
    scores = scores[:, :step_count].reshape(peers, step_count, 2 * group, capacity)
    scores = jnp.transpose(jnp.sum(scores, axis=2), (0, 2, 1))
    return decoded_rows, scores.reshape(1, slots, step_count)


def per_device(step_input, *rest):
    peers = lax.axis_size("dp")
    rows = step_input.shape[0]
    step_count, q_width = step_input.shape[1:]
    resp_slots, kv_width = rest[1].shape[1], rest[1].shape[3]
    fits = (
        rows == 8 * peers
        and rest[2].shape[1] == HD
        and 16 * q_width == HD * kv_width
        and kv_width % (2 * HD) == 0
        and 8 * (resp_slots + step_count) <= HD
        and peers % 2 == 0
        and step_count <= 8
    )
    if fits:
        return per_device_gathered(step_input, *rest)
    return per_device_routed(step_input, *rest)


def solution(mesh):
    in_specs = (
        P(("groups", "dp"), None, "tensor"),
        P(("groups", "dp"), None, None, "tensor"),
        P(("groups", "dp"), None, None, "tensor"),
        P(("groups", "dp"), None, None, "tensor"),
        P(("groups", "dp"), None, None, "tensor"),
        P(("groups", "dp")),
        P(("groups", "dp")),
        P(("groups", "dp")),
        P(("groups", "dp")),
        P("tensor"),
    )
    out_specs = (P(("groups", "dp"), None, "tensor"), P(("groups", "dp"), None, None))
    return jax.shard_map(
        per_device, mesh=mesh, in_specs=in_specs, out_specs=out_specs, check_vma=False
    )
```

```python
import functools
import math

import jax
import jax.numpy as jnp
from jax import lax
from jax.experimental import pallas as pl
from jax.experimental.pallas import tpu as pltpu
from jax.sharding import PartitionSpec as P

HD = 128
LOG2E = 1.4426950408889634


def softmax_pieces(scores, key_valid):
    masked = jnp.where(key_valid, scores, -jnp.inf)
    top_score = jnp.max(masked, axis=-1, keepdims=True)
    weight = jnp.exp(masked - top_score)
    return (weight, jnp.sum(weight, axis=-1), top_score[..., 0])


def per_device_routed(
    step_input,
    new_kv,
    resp_cache,
    policy_prompt,
    ref_prompt,
    prompt_len,
    resp_len,
    row_owner,
    finished,
    probe,
):
    row_count = step_input.shape[0]
    step_count = step_input.shape[1]
    q_width = step_input.shape[2]
    kv_width = new_kv.shape[3]
    q_heads = q_width // HD
    kv_heads = kv_width // HD
    group_size = q_heads // kv_heads
    inv_scale = 1.0 / math.sqrt(HD)
    peer_count = lax.axis_size("dp")
    capacity = max(2, (row_count + peer_count - 1) // peer_count)
    slot_count = peer_count * capacity
    resp_slots = resp_cache.shape[1]
    prompt_width = policy_prompt.shape[1]
    row_iota = jnp.arange(row_count, dtype=jnp.int32)
    same_owner = (row_owner[:, None] == row_owner[None, :]) & (
        row_iota[None, :] < row_iota[:, None]
    )
    slot_index = row_owner * capacity + jnp.sum(same_owner.astype(jnp.int32), axis=1)
    dispatch = slot_index[:, None] == jnp.arange(slot_count, dtype=jnp.int32)[None, :]
    one_hot = dispatch.T

    def to_slots(rows_data):
        picked = jnp.tensordot(one_hot.astype(rows_data.dtype), rows_data, axes=1)
        return picked.reshape((peer_count, capacity) + rows_data.shape[1:])

    live_len = jnp.where(finished == 1, resp_len, 0).astype(jnp.bfloat16)
    own_all = jnp.concatenate([resp_cache, new_kv], axis=1)
    reply_iota = jnp.arange(resp_slots + step_count)
    pol_keys = policy_prompt[0, :, 0].reshape(prompt_width, kv_heads, HD)
    pol_values = policy_prompt[0, :, 1].reshape(prompt_width, kv_heads, HD)
    prompt_valid = jnp.arange(prompt_width) < prompt_len[0]
    resp_keys = own_all[:, :, 0].reshape(row_count, -1, kv_heads, HD)
    resp_values = own_all[:, :, 1].reshape(row_count, -1, kv_heads, HD)
    previous = jnp.zeros((row_count, q_width), jnp.float32)
    decoded_list = []
    query_list = []
    kept_list = []
    for step_idx in range(step_count):
        queries = (step_input[:, step_idx].astype(jnp.float32) + previous).astype(jnp.bfloat16)
        query_list.append(queries)
        received = lax.all_to_all(to_slots(queries), "dp", split_axis=0, concat_axis=0, tiled=True)
        lead_shape = received.shape[:2]
        prompt_queries = received.reshape(-1, kv_heads, group_size, HD)
        scores = (
            jnp.einsum(
                "skgd,tkd->skgt", prompt_queries, pol_keys, preferred_element_type=jnp.float32
            )
            * inv_scale
        )
        prompt_weight, prompt_weight_sum, prompt_top_score = softmax_pieces(scores, prompt_valid)
        prompt_summed = jnp.einsum(
            "skgt,tkd->skgd",
            prompt_weight.astype(jnp.bfloat16),
            pol_values,
            preferred_element_type=jnp.float32,
        )
        part_out = (
            (prompt_summed / prompt_weight_sum[..., None])
            .astype(jnp.bfloat16)
            .reshape(lead_shape + (q_width,))
        )
        part_lse = (prompt_top_score + jnp.log(prompt_weight_sum)).reshape(lead_shape + (q_heads,))
        back_out = lax.all_to_all(part_out, "dp", split_axis=0, concat_axis=0, tiled=True)
        back_lse = lax.all_to_all(part_lse, "dp", split_axis=0, concat_axis=0, tiled=True)
        results = (back_out, back_lse, received)
        back_out = results[0]
        back_lse = results[1]
        kept_list.append(results[2])
        prompt_out = jnp.dot(
            dispatch.astype(jnp.bfloat16),
            back_out.reshape(slot_count, q_width),
            preferred_element_type=jnp.float32,
        )
        prompt_lse = jnp.dot(
            dispatch.astype(jnp.float32),
            back_lse.reshape(slot_count, q_heads),
            precision=lax.Precision.HIGHEST,
        )
        query_heads = queries.reshape(row_count, kv_heads, group_size, HD)
        scores = (
            jnp.einsum(
                "rkgd,rtkd->rkgt", query_heads, resp_keys, preferred_element_type=jnp.float32
            )
            * inv_scale
        )
        reply_valid = jnp.where(
            reply_iota[None, :] < resp_slots,
            reply_iota[None, :] < resp_len[:, None],
            reply_iota[None, :] <= resp_slots + step_idx,
        )
        weight, weight_sum, top_score = softmax_pieces(scores, reply_valid[:, None, None, :])
        summed = jnp.einsum(
            "rkgt,rtkd->rkgd",
            weight.astype(jnp.bfloat16),
            resp_values,
            preferred_element_type=jnp.float32,
        )
        own_out = (summed / weight_sum[..., None]).reshape(row_count, q_heads, HD)
        own_lse = (top_score + jnp.log(weight_sum)).reshape(row_count, q_heads)
        joint_lse = jnp.maximum(prompt_lse, own_lse)
        prompt_wt = jnp.exp(prompt_lse - joint_lse)
        own_wt = jnp.exp(own_lse - joint_lse)
        blended = (
            prompt_wt[..., None] * prompt_out.reshape(row_count, q_heads, HD)
            + own_wt[..., None] * own_out
        ) / (prompt_wt + own_wt)[..., None]
        decoded_now = blended.reshape(row_count, q_width).astype(jnp.bfloat16)
        decoded_list.append(decoded_now)
        previous = lax.optimization_barrier(decoded_now).astype(jnp.float32)
    recv_kv, recv_live = (
        lax.all_to_all(to_slots(own_all), "dp", split_axis=0, concat_axis=0, tiled=True),
        lax.all_to_all(to_slots(live_len), "dp", split_axis=0, concat_axis=0, tiled=True),
    )
    recv_queries = jnp.stack(kept_list, axis=2)
    ref_keys = ref_prompt[0, :, 0].reshape(prompt_width, kv_heads, HD)
    ref_values = ref_prompt[0, :, 1].reshape(prompt_width, kv_heads, HD)
    slot_kv = recv_kv.reshape(slot_count, resp_slots + step_count, 2, kv_width)
    slot_keys = slot_kv[:, :, 0].reshape(slot_count, -1, kv_heads, HD)
    slot_values = slot_kv[:, :, 1].reshape(slot_count, -1, kv_heads, HD)
    slot_len = recv_live.reshape(slot_count).astype(jnp.int32)
    slot_queries = recv_queries.reshape(slot_count, step_count, q_width)
    probe_heads = probe.reshape(kv_heads, group_size, HD)
    prompt_mask = jnp.broadcast_to(prompt_valid[None, :], (slot_count, prompt_width))
    score_list = []
    for step_idx in range(step_count):
        queries = slot_queries[:, step_idx].reshape(slot_count, kv_heads, group_size, HD)
        prompt_scores = (
            jnp.einsum("skgd,tkd->skgt", queries, ref_keys, preferred_element_type=jnp.float32)
            * inv_scale
        )
        reply_scores = (
            jnp.einsum("skgd,stkd->skgt", queries, slot_keys, preferred_element_type=jnp.float32)
            * inv_scale
        )
        reply_valid = jnp.where(
            reply_iota[None, :] < resp_slots,
            reply_iota[None, :] < slot_len[:, None],
            reply_iota[None, :] <= resp_slots + step_idx,
        )
        key_valid = jnp.concatenate([prompt_mask, reply_valid], axis=1)
        weight, weight_sum, top_score = softmax_pieces(
            jnp.concatenate([prompt_scores, reply_scores], axis=-1), key_valid[:, None, None, :]
        )
        weight_low = weight.astype(jnp.bfloat16)
        summed = jnp.einsum(
            "skgt,tkd->skgd",
            weight_low[..., :prompt_width],
            ref_values,
            preferred_element_type=jnp.float32,
        )
        summed = summed + jnp.einsum(
            "skgt,stkd->skgd",
            weight_low[..., prompt_width:],
            slot_values,
            preferred_element_type=jnp.float32,
        )
        ref_out = summed / weight_sum[..., None]
        score_list.append(
            jnp.einsum("skgd,kgd->s", ref_out, probe_heads, precision=lax.Precision.HIGHEST)
        )
    head_terms = jnp.stack(score_list, axis=1)
    head_total = lax.psum(head_terms, "tensor")
    ref_score = jnp.where(slot_len[:, None] > 0, head_total, jnp.zeros((), jnp.float32)).reshape(
        1, slot_count, step_count
    )
    return (jnp.stack(decoded_list, axis=1), ref_score)


def dot_n(a, b):
    return lax.dot_general(a, b, (((1,), (0,)), ((), ())), preferred_element_type=jnp.float32)


def softmax_part(z, valid, both_heads, values_t):
    masked = jnp.where(valid, z, -jnp.inf)
    top = jnp.max(masked, axis=0, keepdims=True)
    weight = jnp.exp2(masked - top)
    total = jnp.sum(weight, axis=0, keepdims=True)
    acc = dot_n(values_t, both_heads(weight.astype(jnp.bfloat16)))
    return top, total, acc


def owner_block(dims, prompt, prompt_len, x_at, kv_at, lens, probe_at, put_decoded, put_score):
    rows, step_count, resp_slots, width, kv_heads, group = dims
    keys_n = resp_slots + step_count
    padded = HD // rows
    lanes = 2 * group * rows
    pairs = kv_heads // 2
    scale = LOG2E / math.sqrt(HD)
    k_iota = lax.broadcasted_iota(jnp.int32, (HD, lanes), 0)
    q_iota = lax.broadcasted_iota(jnp.int32, (HD, lanes), 1)
    prompt_valid = k_iota.astype(jnp.float32) < prompt_len
    same_row = lax.rem(q_iota, rows) == lax.rem(k_iota, rows)
    key_t = lax.div(k_iota, rows)
    cached = same_row & (key_t < resp_slots) & (key_t.astype(jnp.float32) < lens)
    fresh = same_row & (key_t >= resp_slots)
    first = (q_iota < lanes // 2).astype(jnp.float32)
    second = (1.0 - first).astype(jnp.bfloat16)
    first = first.astype(jnp.bfloat16)

    def both_heads(v):
        return jnp.concatenate([v * first, v * second], axis=0)

    blank = [jnp.zeros((rows, HD), jnp.float32)] * (padded - keys_n)

    def stacked(c, k):
        return jnp.concatenate([kv_at(t, c, k) for t in range(keys_n)] + blank, axis=0)

    keys, own_values = [], []
    for p in range(pairs):
        cols = slice(2 * p * HD, 2 * (p + 1) * HD)
        own = [stacked(0, 2 * p + i).astype(jnp.bfloat16) for i in range(2)]
        keys.append(
            jnp.concatenate(
                [prompt(0)[:, cols], prompt(2)[:, cols], jnp.concatenate(own, axis=1)], axis=0
            )
        )
        own = [stacked(1, 2 * p + i).T.astype(jnp.bfloat16) for i in range(2)]
        own_values.append(jnp.concatenate(own, axis=1))
    previous = [None] * pairs
    for s in range(step_count):
        own_valid = cached | (fresh & (key_t <= resp_slots + s))
        score = None
        for p in range(pairs):
            cols = slice(2 * p * HD, 2 * (p + 1) * HD)
            heads = range(2 * p * group, 2 * (p + 1) * group)
            q = jnp.concatenate([x_at(s, h) for h in heads], axis=0).T
            if s > 0:
                q = q + previous[p]
            z = dot_n(keys[p], both_heads(q.astype(jnp.bfloat16))) * scale
            top_p, sum_p, acc_p = softmax_part(
                z[:width], prompt_valid, both_heads, prompt(1)[:, cols]
            )
            top_o, sum_o, acc_o = softmax_part(
                z[2 * width :], own_valid, both_heads, own_values[p]
            )
            prompt_out = (acc_p * (1.0 / sum_p)).astype(jnp.bfloat16).astype(jnp.float32)
            joint = jnp.maximum(top_p, top_o)
            wt_p = sum_p * jnp.exp2(top_p - joint)
            ex_o = jnp.exp2(top_o - joint)
            inv = 1.0 / (wt_p + ex_o * sum_o)
            decoded = (wt_p * inv) * prompt_out + (ex_o * inv) * acc_o
            decoded = decoded.astype(jnp.bfloat16).astype(jnp.float32)
            previous[p] = decoded
            put_decoded(s, p, decoded.T)
            top_r, sum_r, acc_r = softmax_part(
                z[width : 2 * width], prompt_valid, both_heads, prompt(3)[:, cols]
            )
            joint = jnp.maximum(top_r, top_o)
            ex_r = jnp.exp2(top_r - joint)
            ex_o = jnp.exp2(top_o - joint)
            inv = 1.0 / (ex_r * sum_r + ex_o * sum_o)
            probe = probe_at(p)
            term = (ex_r * inv) * jnp.sum(acc_r * probe, axis=0, keepdims=True)
            term = term + (ex_o * inv) * jnp.sum(acc_o * probe, axis=0, keepdims=True)
            score = term if score is None else score + term
        put_score(s, score)


def place_rows(dims, owners, row_ref, lane_scr):
    rows, _, _, _, _, group = dims
    owner = row_ref[0:1, :]
    count = owner.shape[1]
    sub = lax.broadcasted_iota(jnp.int32, (count, count), 0)
    lane = lax.broadcasted_iota(jnp.int32, (count, count), 1)

    def column(row):
        return jnp.sum(jnp.where(sub == lane, row, 0), axis=1, keepdims=True)

    same = (column(owner) == owner) & (sub < lane)
    rank = jnp.sum(jnp.where(same, 1, 0), axis=0, keepdims=True)
    slot = owner * rows + rank
    row_at = jnp.where(sub == slot, 1.0, 0.0).astype(jnp.bfloat16)
    slot_at = jnp.where(column(slot) == lane, 1.0, 0.0).astype(jnp.bfloat16)
    lanes = 2 * group * rows
    of_lane = lax.rem(lax.broadcasted_iota(jnp.int32, (count, lanes), 1), rows)
    spread = jnp.where(column(rank) == of_lane, 1.0, 0.0).astype(jnp.bfloat16)
    owner_id = lax.broadcasted_iota(jnp.int32, (owners, count), 0)
    for i in range(2):
        value = row_ref[i + 1 : i + 2, :].astype(jnp.float32)
        mine = jnp.where(owner_id == owner, value, 0.0).astype(jnp.bfloat16)
        lane_scr[i] = dot_n(mine, spread)
    return row_at, slot_at


def fused_kernel(
    dims,
    pol_ref,
    ref_ref,
    plen_ref,
    x_ref,
    cache_ref,
    new_ref,
    row_ref,
    probe_ref,
    dec_ref,
    score_ref,
    buf,
    x_scr,
    kv_scr,
    dec_scr,
    lane_scr,
    probe_scr,
    mail,
    got,
    send_sem,
    recv_sem,
    mail_send,
    mail_recv,
):
    rows, step_count, resp_slots, width, kv_heads, group = dims
    n = buf.shape[0]
    half = n // 2
    tensors = got.shape[0]
    part = lax.axis_index("groups")
    me = lax.axis_index("dp")
    tau = lax.axis_index("tensor")
    z = lax.div(me, 2)
    y = lax.rem(me, 2)

    def device(dp, t):
        return (part, dp, t)

    barrier = pltpu.get_barrier_semaphore()
    for dt in range(tensors):
        for j in range(n):
            if dt or j:
                pl.semaphore_signal(
                    barrier,
                    inc=1,
                    device_id=device(lax.rem(me + j, n), lax.rem(tau + dt, tensors)),
                    device_id_type=pl.DeviceIdType.MESH,
                )
    pl.semaphore_wait(barrier, tensors * n - 1)

    across = me + 1 - 2 * y
    targets = (jnp.minimum(me + 2, n - 2 + y), jnp.maximum(me - 2, y), across)

    def hop(src, o, way):
        return pltpu.make_async_remote_copy(
            src_ref=src,
            dst_ref=buf.at[o],
            send_sem=send_sem.at[way, o],
            recv_sem=recv_sem.at[o],
            device_id=device(targets[way], tau),
            device_id_type=pl.DeviceIdType.MESH,
        )

    def each_way(zz, act):
        o = 2 * zz + y
        pl.when((z < half - 1) & (zz <= z))(lambda: act(o, 0))
        pl.when((z > 0) & (zz >= z))(lambda: act(o, 1))
        act(o, 2)

    for i, prompt_ref in enumerate((pol_ref, ref_ref)):
        top = 2 * i * width
        buf[me, top : top + width, :] = prompt_ref[0]
        for k in range(kv_heads):
            cols = slice(k * HD, (k + 1) * HD)
            turned = prompt_ref[1, :, cols].astype(jnp.float32).T
            buf[me, top + width : top + 2 * width, cols] = turned.astype(jnp.bfloat16)
    plen = jnp.broadcast_to(plen_ref[0:1, :].astype(jnp.float32), (16, HD))
    for k in range(kv_heads):
        buf[me, 4 * width :, k * HD : (k + 1) * HD] = plen.astype(jnp.bfloat16)
    each_way(z, lambda o, way: hop(buf.at[o], o, way).start())
    row_at, slot_at = place_rows(dims, n, row_ref, lane_scr)
    pairs = kv_heads // 2
    for p in range(pairs):
        by_head = probe_ref[2 * p * group : 2 * (p + 1) * group]
        spread = jnp.concatenate(
            [jnp.broadcast_to(by_head[i : i + 1], (rows, HD)) for i in range(2 * group)], axis=0
        )
        probe_scr[p] = spread.T
    for t in range(resp_slots + step_count):
        for c in range(2):
            held = cache_ref[t, c] if t < resp_slots else new_ref[t - resp_slots, c]
            kv_scr[t, c] = dot_n(row_at, held)

    def place_x(s, carry):
        x_scr[s] = dot_n(row_at, x_ref[s])
        return carry

    lax.fori_loop(0, step_count, place_x, 0)

    def by_distance(i):
        up, down = half - 1 - z, z
        near = jnp.minimum(up, down)
        paired = lax.div(i + 1, 2) * jnp.where(lax.rem(i, 2) == 1, 1, -1)
        beyond = (i - near) * jnp.where(up > down, 1, -1)
        return z + jnp.where(i <= 2 * near, paired, beyond)

    def letter(o, dt):
        return pltpu.make_async_remote_copy(
            src_ref=mail.at[o],
            dst_ref=got.at[tau, me],
            send_sem=mail_send.at[dt, o],
            recv_sem=mail_recv.at[tau, me],
            device_id=device(o, lax.rem(tau + dt, tensors)),
            device_id_type=pl.DeviceIdType.MESH,
        )

    def turn(t, carry):
        odd = lax.rem(t, 2) == 1
        last = t == n - 1
        line = (t == 0) | (odd & jnp.logical_not(last))
        order = jnp.where(
            line, lax.div(t + 1, 2), jnp.where(last, half - 1, lax.div(t, 2) - 1)
        )
        zz = by_distance(order)
        o = 2 * zz + jnp.where(line, y, 1 - y)

        @pl.when(t > 0)
        def _():
            hop(buf.at[o], o, 2).wait_recv()

        @pl.when((t > 0) & line)
        def _():
            each_way(zz, lambda b, way: hop(buf.at[b], b, way).start())

        here = pl.ds(pl.multiple_of(o * rows, rows), rows)

        def put_decoded(s, p, decoded):
            for i in range(2 * group):
                h = 2 * p * group + i
                dec_scr[s, here, h * HD : (h + 1) * HD] = decoded[i * rows : (i + 1) * rows]

        def put_score(s, score):
            mail[o, s : s + 1, :] = jnp.where(lane_scr[1, pl.ds(o, 1), :] > 0.5, score, 0.0)

        owner_block(
            dims,
            lambda i: buf[o, i * width : (i + 1) * width, :],
            buf[o, 4 * width :, :HD][0:1].astype(jnp.float32),
            lambda s, h: x_scr[s, here, h * HD : (h + 1) * HD],
            lambda t, c, k: kv_scr[t, c, here, k * HD : (k + 1) * HD],
            lane_scr[0, pl.ds(o, 1), :],
            lambda p: probe_scr[p],
            put_decoded,
            put_score,
        )
        for dt in range(1, tensors):
            letter(o, dt).start()
        pl.when(o != me)(lambda: letter(o, 0).start())

        @pl.when(o == me)
        def _():
            got[tau, me] = mail[me]

        return carry

    mail[...] = jnp.zeros_like(mail)
    lax.fori_loop(0, n, turn, 0)

    def place_decoded(s, carry):
        dec_ref[s] = dot_n(slot_at, dec_scr[s].astype(jnp.bfloat16)).astype(jnp.bfloat16)
        return carry

    lax.fori_loop(0, step_count, place_decoded, 0)

    def arrived(t, b):
        return pltpu.make_async_remote_copy(
            src_ref=mail.at[b],
            dst_ref=got.at[t, b],
            send_sem=mail_send.at[0, b],
            recv_sem=mail_recv.at[t, b],
            device_id=device(across, tau),
            device_id_type=pl.DeviceIdType.MESH,
        )

    def finish(b, carry):
        for dt in range(1, tensors):
            arrived(lax.rem(tau + dt, tensors), b).wait_recv()
            letter(b, dt).wait_send()

        @pl.when(b != me)
        def _():
            arrived(tau, b).wait_recv()
            letter(b, 0).wait_send()

        return carry

    lax.fori_loop(0, n, finish, 0)

    def sent(zz, carry):
        each_way(zz, lambda o, way: hop(buf.at[o], o, way).wait_send())
        return carry

    lax.fori_loop(0, half, sent, 0)
    total = got[0]
    for t in range(1, tensors):
        total = total + got[t]
    score_ref[...] = total


def per_device_gathered(
    step_input,
    new_kv,
    resp_cache,
    policy_prompt,
    ref_prompt,
    prompt_len,
    resp_len,
    row_owner,
    finished,
    probe,
):
    row_count, step_count, q_width = step_input.shape
    kv_width = new_kv.shape[3]
    q_heads = q_width // HD
    kv_heads = kv_width // HD
    group = q_heads // kv_heads
    peers = lax.axis_size("dp")
    capacity = max(2, (row_count + peers - 1) // peers)
    slots = peers * capacity
    resp_slots = resp_cache.shape[1]
    keys_n = resp_slots + step_count
    width = policy_prompt.shape[1]
    lanes = 2 * group * capacity
    pairs = kv_heads // 2
    dims = (capacity, step_count, resp_slots, width, kv_heads, group)

    tensors = lax.axis_size("tensor")
    vmem = pl.BlockSpec(memory_space=pltpu.VMEM)
    decoded, scores = pl.pallas_call(
        functools.partial(fused_kernel, dims),
        in_specs=[vmem] * 8,
        out_specs=[vmem] * 2,
        out_shape=[
            jax.ShapeDtypeStruct((step_count, row_count, q_width), jnp.bfloat16),
            jax.ShapeDtypeStruct((peers, 8, lanes), jnp.float32),
        ],
        scratch_shapes=[
            pltpu.VMEM((peers, 4 * width + 16, kv_width), jnp.bfloat16),
            pltpu.VMEM((step_count, slots, q_width), jnp.float32),
            pltpu.VMEM((keys_n, 2, slots, kv_width), jnp.float32),
            pltpu.VMEM((step_count, slots, q_width), jnp.float32),
            pltpu.VMEM((2, peers, lanes), jnp.float32),
            pltpu.VMEM((pairs, HD, lanes), jnp.float32),
            pltpu.VMEM((peers, 8, lanes), jnp.float32),
            pltpu.VMEM((tensors, peers, 8, lanes), jnp.float32),
            pltpu.SemaphoreType.DMA((3, peers)),
            pltpu.SemaphoreType.DMA((peers,)),
            pltpu.SemaphoreType.DMA((tensors, peers)),
            pltpu.SemaphoreType.DMA((tensors, peers)),
        ],
        compiler_params=pltpu.CompilerParams(
            collective_id=0, has_side_effects=True, vmem_limit_bytes=48 * 1024 * 1024
        ),
    )(
        jnp.transpose(policy_prompt[0], (1, 0, 2)),
        jnp.transpose(ref_prompt[0], (1, 0, 2)),
        jnp.broadcast_to(prompt_len[:, None], (8, HD)),
        jnp.transpose(step_input, (1, 0, 2)),
        jnp.transpose(resp_cache, (1, 2, 0, 3)),
        jnp.transpose(new_kv, (1, 2, 0, 3)),
        jnp.stack([row_owner, resp_len, finished] + [finished] * 5),
        probe.reshape(q_heads, HD),
    )
    decoded_rows = jnp.transpose(decoded, (1, 0, 2))
    scores = scores[:, :step_count].reshape(peers, step_count, 2 * group, capacity)
    scores = jnp.transpose(jnp.sum(scores, axis=2), (0, 2, 1))
    return decoded_rows, scores.reshape(1, slots, step_count)


def per_device(step_input, *rest):
    peers = lax.axis_size("dp")
    rows = step_input.shape[0]
    step_count, q_width = step_input.shape[1:]
    resp_slots, kv_width = rest[1].shape[1], rest[1].shape[3]
    fits = (
        rows == 8 * peers
        and rest[2].shape[1] == HD
        and 16 * q_width == HD * kv_width
        and kv_width % (2 * HD) == 0
        and 8 * (resp_slots + step_count) <= HD
        and peers % 2 == 0
        and step_count <= 8
    )
    if fits:
        return per_device_gathered(step_input, *rest)
    return per_device_routed(step_input, *rest)


def solution(mesh):
    in_specs = (
        P(("groups", "dp"), None, "tensor"),
        P(("groups", "dp"), None, None, "tensor"),
        P(("groups", "dp"), None, None, "tensor"),
        P(("groups", "dp"), None, None, "tensor"),
        P(("groups", "dp"), None, None, "tensor"),
        P(("groups", "dp")),
        P(("groups", "dp")),
        P(("groups", "dp")),
        P(("groups", "dp")),
        P("tensor"),
    )
    out_specs = (P(("groups", "dp"), None, "tensor"), P(("groups", "dp"), None, None))
    return jax.shard_map(
        per_device, mesh=mesh, in_specs=in_specs, out_specs=out_specs, check_vma=False
    )
```

```python
import functools
import math

import jax
import jax.numpy as jnp
from jax import lax
from jax.experimental import pallas as pl
from jax.experimental.pallas import tpu as pltpu
from jax.sharding import PartitionSpec as P

HD = 128
LOG2E = 1.4426950408889634


def softmax_pieces(scores, key_valid):
    masked = jnp.where(key_valid, scores, -jnp.inf)
    top_score = jnp.max(masked, axis=-1, keepdims=True)
    weight = jnp.exp(masked - top_score)
    return (weight, jnp.sum(weight, axis=-1), top_score[..., 0])


def per_device_routed(
    step_input,
    new_kv,
    resp_cache,
    policy_prompt,
    ref_prompt,
    prompt_len,
    resp_len,
    row_owner,
    finished,
    probe,
):
    row_count = step_input.shape[0]
    step_count = step_input.shape[1]
    q_width = step_input.shape[2]
    kv_width = new_kv.shape[3]
    q_heads = q_width // HD
    kv_heads = kv_width // HD
    group_size = q_heads // kv_heads
    inv_scale = 1.0 / math.sqrt(HD)
    peer_count = lax.axis_size("dp")
    capacity = max(2, (row_count + peer_count - 1) // peer_count)
    slot_count = peer_count * capacity
    resp_slots = resp_cache.shape[1]
    prompt_width = policy_prompt.shape[1]
    row_iota = jnp.arange(row_count, dtype=jnp.int32)
    same_owner = (row_owner[:, None] == row_owner[None, :]) & (
        row_iota[None, :] < row_iota[:, None]
    )
    slot_index = row_owner * capacity + jnp.sum(same_owner.astype(jnp.int32), axis=1)
    dispatch = slot_index[:, None] == jnp.arange(slot_count, dtype=jnp.int32)[None, :]
    one_hot = dispatch.T

    def to_slots(rows_data):
        picked = jnp.tensordot(one_hot.astype(rows_data.dtype), rows_data, axes=1)
        return picked.reshape((peer_count, capacity) + rows_data.shape[1:])

    live_len = jnp.where(finished == 1, resp_len, 0).astype(jnp.bfloat16)
    own_all = jnp.concatenate([resp_cache, new_kv], axis=1)
    reply_iota = jnp.arange(resp_slots + step_count)
    pol_keys = policy_prompt[0, :, 0].reshape(prompt_width, kv_heads, HD)
    pol_values = policy_prompt[0, :, 1].reshape(prompt_width, kv_heads, HD)
    prompt_valid = jnp.arange(prompt_width) < prompt_len[0]
    resp_keys = own_all[:, :, 0].reshape(row_count, -1, kv_heads, HD)
    resp_values = own_all[:, :, 1].reshape(row_count, -1, kv_heads, HD)
    previous = jnp.zeros((row_count, q_width), jnp.float32)
    decoded_list = []
    query_list = []
    kept_list = []
    for step_idx in range(step_count):
        queries = (step_input[:, step_idx].astype(jnp.float32) + previous).astype(jnp.bfloat16)
        query_list.append(queries)
        received = lax.all_to_all(to_slots(queries), "dp", split_axis=0, concat_axis=0, tiled=True)
        lead_shape = received.shape[:2]
        prompt_queries = received.reshape(-1, kv_heads, group_size, HD)
        scores = (
            jnp.einsum(
                "skgd,tkd->skgt", prompt_queries, pol_keys, preferred_element_type=jnp.float32
            )
            * inv_scale
        )
        prompt_weight, prompt_weight_sum, prompt_top_score = softmax_pieces(scores, prompt_valid)
        prompt_summed = jnp.einsum(
            "skgt,tkd->skgd",
            prompt_weight.astype(jnp.bfloat16),
            pol_values,
            preferred_element_type=jnp.float32,
        )
        part_out = (
            (prompt_summed / prompt_weight_sum[..., None])
            .astype(jnp.bfloat16)
            .reshape(lead_shape + (q_width,))
        )
        part_lse = (prompt_top_score + jnp.log(prompt_weight_sum)).reshape(lead_shape + (q_heads,))
        back_out = lax.all_to_all(part_out, "dp", split_axis=0, concat_axis=0, tiled=True)
        back_lse = lax.all_to_all(part_lse, "dp", split_axis=0, concat_axis=0, tiled=True)
        results = (back_out, back_lse, received)
        back_out = results[0]
        back_lse = results[1]
        kept_list.append(results[2])
        prompt_out = jnp.dot(
            dispatch.astype(jnp.bfloat16),
            back_out.reshape(slot_count, q_width),
            preferred_element_type=jnp.float32,
        )
        prompt_lse = jnp.dot(
            dispatch.astype(jnp.float32),
            back_lse.reshape(slot_count, q_heads),
            precision=lax.Precision.HIGHEST,
        )
        query_heads = queries.reshape(row_count, kv_heads, group_size, HD)
        scores = (
            jnp.einsum(
                "rkgd,rtkd->rkgt", query_heads, resp_keys, preferred_element_type=jnp.float32
            )
            * inv_scale
        )
        reply_valid = jnp.where(
            reply_iota[None, :] < resp_slots,
            reply_iota[None, :] < resp_len[:, None],
            reply_iota[None, :] <= resp_slots + step_idx,
        )
        weight, weight_sum, top_score = softmax_pieces(scores, reply_valid[:, None, None, :])
        summed = jnp.einsum(
            "rkgt,rtkd->rkgd",
            weight.astype(jnp.bfloat16),
            resp_values,
            preferred_element_type=jnp.float32,
        )
        own_out = (summed / weight_sum[..., None]).reshape(row_count, q_heads, HD)
        own_lse = (top_score + jnp.log(weight_sum)).reshape(row_count, q_heads)
        joint_lse = jnp.maximum(prompt_lse, own_lse)
        prompt_wt = jnp.exp(prompt_lse - joint_lse)
        own_wt = jnp.exp(own_lse - joint_lse)
        blended = (
            prompt_wt[..., None] * prompt_out.reshape(row_count, q_heads, HD)
            + own_wt[..., None] * own_out
        ) / (prompt_wt + own_wt)[..., None]
        decoded_now = blended.reshape(row_count, q_width).astype(jnp.bfloat16)
        decoded_list.append(decoded_now)
        previous = lax.optimization_barrier(decoded_now).astype(jnp.float32)
    recv_kv, recv_live = (
        lax.all_to_all(to_slots(own_all), "dp", split_axis=0, concat_axis=0, tiled=True),
        lax.all_to_all(to_slots(live_len), "dp", split_axis=0, concat_axis=0, tiled=True),
    )
    recv_queries = jnp.stack(kept_list, axis=2)
    ref_keys = ref_prompt[0, :, 0].reshape(prompt_width, kv_heads, HD)
    ref_values = ref_prompt[0, :, 1].reshape(prompt_width, kv_heads, HD)
    slot_kv = recv_kv.reshape(slot_count, resp_slots + step_count, 2, kv_width)
    slot_keys = slot_kv[:, :, 0].reshape(slot_count, -1, kv_heads, HD)
    slot_values = slot_kv[:, :, 1].reshape(slot_count, -1, kv_heads, HD)
    slot_len = recv_live.reshape(slot_count).astype(jnp.int32)
    slot_queries = recv_queries.reshape(slot_count, step_count, q_width)
    probe_heads = probe.reshape(kv_heads, group_size, HD)
    prompt_mask = jnp.broadcast_to(prompt_valid[None, :], (slot_count, prompt_width))
    score_list = []
    for step_idx in range(step_count):
        queries = slot_queries[:, step_idx].reshape(slot_count, kv_heads, group_size, HD)
        prompt_scores = (
            jnp.einsum("skgd,tkd->skgt", queries, ref_keys, preferred_element_type=jnp.float32)
            * inv_scale
        )
        reply_scores = (
            jnp.einsum("skgd,stkd->skgt", queries, slot_keys, preferred_element_type=jnp.float32)
            * inv_scale
        )
        reply_valid = jnp.where(
            reply_iota[None, :] < resp_slots,
            reply_iota[None, :] < slot_len[:, None],
            reply_iota[None, :] <= resp_slots + step_idx,
        )
        key_valid = jnp.concatenate([prompt_mask, reply_valid], axis=1)
        weight, weight_sum, top_score = softmax_pieces(
            jnp.concatenate([prompt_scores, reply_scores], axis=-1), key_valid[:, None, None, :]
        )
        weight_low = weight.astype(jnp.bfloat16)
        summed = jnp.einsum(
            "skgt,tkd->skgd",
            weight_low[..., :prompt_width],
            ref_values,
            preferred_element_type=jnp.float32,
        )
        summed = summed + jnp.einsum(
            "skgt,stkd->skgd",
            weight_low[..., prompt_width:],
            slot_values,
            preferred_element_type=jnp.float32,
        )
        ref_out = summed / weight_sum[..., None]
        score_list.append(
            jnp.einsum("skgd,kgd->s", ref_out, probe_heads, precision=lax.Precision.HIGHEST)
        )
    head_terms = jnp.stack(score_list, axis=1)
    head_total = lax.psum(head_terms, "tensor")
    ref_score = jnp.where(slot_len[:, None] > 0, head_total, jnp.zeros((), jnp.float32)).reshape(
        1, slot_count, step_count
    )
    return (jnp.stack(decoded_list, axis=1), ref_score)


def dot_n(a, b):
    return lax.dot_general(a, b, (((1,), (0,)), ((), ())), preferred_element_type=jnp.float32)


def softmax_part(z, valid, both_heads, values_t):
    masked = jnp.where(valid, z, -jnp.inf)
    top = jnp.max(masked, axis=0, keepdims=True)
    weight = jnp.exp2(masked - top)
    total = jnp.sum(weight, axis=0, keepdims=True)
    acc = dot_n(values_t, both_heads(weight.astype(jnp.bfloat16)))
    return top, total, acc


def owner_block(dims, prompt, prompt_len, x_at, kv_at, lens, probe_at, put_decoded, put_score):
    rows, step_count, resp_slots, width, kv_heads, group = dims
    keys_n = resp_slots + step_count
    padded = HD // rows
    lanes = 2 * group * rows
    pairs = kv_heads // 2
    scale = LOG2E / math.sqrt(HD)
    k_iota = lax.broadcasted_iota(jnp.int32, (HD, lanes), 0)
    q_iota = lax.broadcasted_iota(jnp.int32, (HD, lanes), 1)
    prompt_valid = k_iota.astype(jnp.float32) < prompt_len
    same_row = lax.rem(q_iota, rows) == lax.rem(k_iota, rows)
    key_t = lax.div(k_iota, rows)
    cached = same_row & (key_t < resp_slots) & (key_t.astype(jnp.float32) < lens)
    fresh = same_row & (key_t >= resp_slots)
    first = (q_iota < lanes // 2).astype(jnp.float32)
    second = (1.0 - first).astype(jnp.bfloat16)
    first = first.astype(jnp.bfloat16)

    def both_heads(v):
        return jnp.concatenate([v * first, v * second], axis=0)

    blank = [jnp.zeros((rows, HD), jnp.float32)] * (padded - keys_n)

    def stacked(c, k):
        return jnp.concatenate([kv_at(t, c, k) for t in range(keys_n)] + blank, axis=0)

    keys, own_values = [], []
    for p in range(pairs):
        cols = slice(2 * p * HD, 2 * (p + 1) * HD)
        own = [stacked(0, 2 * p + i).astype(jnp.bfloat16) for i in range(2)]
        keys.append(
            jnp.concatenate(
                [prompt(0)[:, cols], prompt(2)[:, cols], jnp.concatenate(own, axis=1)], axis=0
            )
        )
        own = [stacked(1, 2 * p + i).T.astype(jnp.bfloat16) for i in range(2)]
        own_values.append(jnp.concatenate(own, axis=1))
    previous = [None] * pairs
    for s in range(step_count):
        own_valid = cached | (fresh & (key_t <= resp_slots + s))
        score = None
        for p in range(pairs):
            cols = slice(2 * p * HD, 2 * (p + 1) * HD)
            heads = range(2 * p * group, 2 * (p + 1) * group)
            q = jnp.concatenate([x_at(s, h) for h in heads], axis=0).T
            if s > 0:
                q = q + previous[p]
            z = dot_n(keys[p], both_heads(q.astype(jnp.bfloat16))) * scale
            top_p, sum_p, acc_p = softmax_part(
                z[:width], prompt_valid, both_heads, prompt(1)[:, cols]
            )
            top_o, sum_o, acc_o = softmax_part(
                z[2 * width :], own_valid, both_heads, own_values[p]
            )
            prompt_out = (acc_p * (1.0 / sum_p)).astype(jnp.bfloat16).astype(jnp.float32)
            joint = jnp.maximum(top_p, top_o)
            wt_p = sum_p * jnp.exp2(top_p - joint)
            ex_o = jnp.exp2(top_o - joint)
            inv = 1.0 / (wt_p + ex_o * sum_o)
            decoded = (wt_p * inv) * prompt_out + (ex_o * inv) * acc_o
            decoded = decoded.astype(jnp.bfloat16).astype(jnp.float32)
            previous[p] = decoded
            put_decoded(s, p, decoded.T)
            top_r, sum_r, acc_r = softmax_part(
                z[width : 2 * width], prompt_valid, both_heads, prompt(3)[:, cols]
            )
            joint = jnp.maximum(top_r, top_o)
            ex_r = jnp.exp2(top_r - joint)
            ex_o = jnp.exp2(top_o - joint)
            inv = 1.0 / (ex_r * sum_r + ex_o * sum_o)
            probe = probe_at(p)
            term = (ex_r * inv) * jnp.sum(acc_r * probe, axis=0, keepdims=True)
            term = term + (ex_o * inv) * jnp.sum(acc_o * probe, axis=0, keepdims=True)
            score = term if score is None else score + term
        put_score(s, score)


def place_rows(dims, owners, row_ref, lane_scr):
    rows, _, _, _, _, group = dims
    owner = row_ref[0:1, :]
    count = owner.shape[1]
    sub = lax.broadcasted_iota(jnp.int32, (count, count), 0)
    lane = lax.broadcasted_iota(jnp.int32, (count, count), 1)

    def column(row):
        return jnp.sum(jnp.where(sub == lane, row, 0), axis=1, keepdims=True)

    same = (column(owner) == owner) & (sub < lane)
    rank = jnp.sum(jnp.where(same, 1, 0), axis=0, keepdims=True)
    slot = owner * rows + rank
    row_at = jnp.where(sub == slot, 1.0, 0.0).astype(jnp.bfloat16)
    slot_at = jnp.where(column(slot) == lane, 1.0, 0.0).astype(jnp.bfloat16)
    lanes = 2 * group * rows
    of_lane = lax.rem(lax.broadcasted_iota(jnp.int32, (count, lanes), 1), rows)
    spread = jnp.where(column(rank) == of_lane, 1.0, 0.0).astype(jnp.bfloat16)
    owner_id = lax.broadcasted_iota(jnp.int32, (owners, count), 0)
    for i in range(2):
        value = row_ref[i + 1 : i + 2, :].astype(jnp.float32)
        mine = jnp.where(owner_id == owner, value, 0.0).astype(jnp.bfloat16)
        lane_scr[i] = dot_n(mine, spread)
    return row_at, slot_at


def fused_kernel(
    dims,
    pol_ref,
    ref_ref,
    plen_ref,
    x_ref,
    cache_ref,
    new_ref,
    row_ref,
    probe_ref,
    dec_ref,
    score_ref,
    buf,
    x_scr,
    kv_scr,
    dec_scr,
    lane_scr,
    probe_scr,
    mail,
    got,
    send_sem,
    recv_sem,
    tail_send,
    tail_recv,
    mail_send,
    mail_recv,
):
    rows, step_count, resp_slots, width, kv_heads, group = dims
    n = buf.shape[0]
    half = n // 2
    tensors = got.shape[0]
    part = lax.axis_index("groups")
    me = lax.axis_index("dp")
    tau = lax.axis_index("tensor")
    z = lax.div(me, 2)
    y = lax.rem(me, 2)

    def device(dp, t):
        return (part, dp, t)

    barrier = pltpu.get_barrier_semaphore()
    for dt in range(tensors):
        for j in range(n):
            if dt or j:
                pl.semaphore_signal(
                    barrier,
                    inc=1,
                    device_id=device(lax.rem(me + j, n), lax.rem(tau + dt, tensors)),
                    device_id_type=pl.DeviceIdType.MESH,
                )
    pl.semaphore_wait(barrier, tensors * n - 1)

    across = me + 1 - 2 * y
    targets = (jnp.minimum(me + 2, n - 2 + y), jnp.maximum(me - 2, y), across)

    def hop(src, o, way):
        return pltpu.make_async_remote_copy(
            src_ref=src,
            dst_ref=buf.at[o],
            send_sem=send_sem.at[way, o],
            recv_sem=recv_sem.at[o],
            device_id=device(targets[way], tau),
            device_id_type=pl.DeviceIdType.MESH,
        )

    next_z = z + 1 - 2 * lax.rem(z, 2)
    cut = 2 * width

    def short_hop(o):
        head = buf.at[o, pl.ds(0, cut)]
        return pltpu.make_async_remote_copy(
            src_ref=head,
            dst_ref=head,
            send_sem=send_sem.at[2, o],
            recv_sem=recv_sem.at[o],
            device_id=device(across, tau),
            device_id_type=pl.DeviceIdType.MESH,
        )

    def tail_hop(o):
        tail = buf.at[o, pl.ds(cut, buf.shape[1] - cut)]
        return pltpu.make_async_remote_copy(
            src_ref=tail,
            dst_ref=tail,
            send_sem=tail_send,
            recv_sem=tail_recv,
            device_id=device(2 * next_z + y, tau),
            device_id_type=pl.DeviceIdType.MESH,
        )

    def each_way(zz, act, act_short):
        o = 2 * zz + y
        pl.when((z < half - 1) & (zz <= z))(lambda: act(o, 0))
        pl.when((z > 0) & (zz >= z))(lambda: act(o, 1))
        pl.when(zz == next_z)(lambda: act_short(o))
        pl.when(zz != next_z)(lambda: act(o, 2))

    for i, prompt_ref in enumerate((pol_ref, ref_ref)):
        top = 2 * i * width
        buf[me, top : top + width, :] = prompt_ref[0]
        for k in range(kv_heads):
            cols = slice(k * HD, (k + 1) * HD)
            turned = prompt_ref[1, :, cols].astype(jnp.float32).T
            buf[me, top + width : top + 2 * width, cols] = turned.astype(jnp.bfloat16)
    plen = jnp.broadcast_to(plen_ref[0:1, :].astype(jnp.float32), (16, HD))
    for k in range(kv_heads):
        buf[me, 4 * width :, k * HD : (k + 1) * HD] = plen.astype(jnp.bfloat16)
    each_way(z, lambda o, way: hop(buf.at[o], o, way).start(), lambda o: short_hop(o).start())
    row_at, slot_at = place_rows(dims, n, row_ref, lane_scr)
    pairs = kv_heads // 2
    for p in range(pairs):
        by_head = probe_ref[2 * p * group : 2 * (p + 1) * group]
        spread = jnp.concatenate(
            [jnp.broadcast_to(by_head[i : i + 1], (rows, HD)) for i in range(2 * group)], axis=0
        )
        probe_scr[p] = spread.T
    for t in range(resp_slots + step_count):
        for c in range(2):
            held = cache_ref[t, c] if t < resp_slots else new_ref[t - resp_slots, c]
            kv_scr[t, c] = dot_n(row_at, held)

    def place_x(s, carry):
        x_scr[s] = dot_n(row_at, x_ref[s])
        return carry

    lax.fori_loop(0, step_count, place_x, 0)

    def by_distance(i):
        up, down = half - 1 - z, z
        near = jnp.minimum(up, down)
        paired = lax.div(i + 1, 2) * jnp.where(lax.rem(i, 2) == 1, 1, -1)
        beyond = (i - near) * jnp.where(up > down, 1, -1)
        return z + jnp.where(i <= 2 * near, paired, beyond)

    def letter(o, dt):
        return pltpu.make_async_remote_copy(
            src_ref=mail.at[o],
            dst_ref=got.at[tau, me],
            send_sem=mail_send.at[dt, o],
            recv_sem=mail_recv.at[tau, me],
            device_id=device(o, lax.rem(tau + dt, tensors)),
            device_id_type=pl.DeviceIdType.MESH,
        )

    def turn(t, carry):
        odd = lax.rem(t, 2) == 1
        last = t == n - 1
        line = (t == 0) | (odd & jnp.logical_not(last))
        order = jnp.where(
            line, lax.div(t + 1, 2), jnp.where(last, half - 1, lax.div(t, 2) - 1)
        )
        zz = by_distance(order)
        o = 2 * zz + jnp.where(line, y, 1 - y)

        in_two = jnp.logical_not(line) & (zz == next_z)

        @pl.when((t > 0) & jnp.logical_not(in_two))
        def _():
            hop(buf.at[o], o, 2).wait_recv()

        @pl.when(in_two)
        def _():
            short_hop(o).wait_recv()
            tail_hop(o).wait_recv()

        @pl.when((t > 0) & line)
        def _():
            each_way(
                zz,
                lambda b, way: hop(buf.at[b], b, way).start(),
                lambda b: short_hop(b).start(),
            )

        @pl.when(jnp.logical_not(line) & (zz == z))
        def _():
            tail_hop(o).start()

        here = pl.ds(pl.multiple_of(o * rows, rows), rows)

        def put_decoded(s, p, decoded):
            for i in range(2 * group):
                h = 2 * p * group + i
                dec_scr[s, here, h * HD : (h + 1) * HD] = decoded[i * rows : (i + 1) * rows]

        def put_score(s, score):
            mail[o, s : s + 1, :] = jnp.where(lane_scr[1, pl.ds(o, 1), :] > 0.5, score, 0.0)

        owner_block(
            dims,
            lambda i: buf[o, i * width : (i + 1) * width, :],
            buf[o, 4 * width :, :HD][0:1].astype(jnp.float32),
            lambda s, h: x_scr[s, here, h * HD : (h + 1) * HD],
            lambda t, c, k: kv_scr[t, c, here, k * HD : (k + 1) * HD],
            lane_scr[0, pl.ds(o, 1), :],
            lambda p: probe_scr[p],
            put_decoded,
            put_score,
        )
        for dt in range(1, tensors):
            letter(o, dt).start()
        pl.when(o != me)(lambda: letter(o, 0).start())

        @pl.when(o == me)
        def _():
            got[tau, me] = mail[me]

        return carry

    mail[...] = jnp.zeros_like(mail)
    lax.fori_loop(0, n, turn, 0)

    def place_decoded(s, carry):
        dec_ref[s] = dot_n(slot_at, dec_scr[s].astype(jnp.bfloat16)).astype(jnp.bfloat16)
        return carry

    lax.fori_loop(0, step_count, place_decoded, 0)

    def arrived(t, b):
        return pltpu.make_async_remote_copy(
            src_ref=mail.at[b],
            dst_ref=got.at[t, b],
            send_sem=mail_send.at[0, b],
            recv_sem=mail_recv.at[t, b],
            device_id=device(across, tau),
            device_id_type=pl.DeviceIdType.MESH,
        )

    def finish(b, carry):
        for dt in range(1, tensors):
            arrived(lax.rem(tau + dt, tensors), b).wait_recv()
            letter(b, dt).wait_send()

        @pl.when(b != me)
        def _():
            arrived(tau, b).wait_recv()
            letter(b, 0).wait_send()

        return carry

    lax.fori_loop(0, n, finish, 0)

    def sent(zz, carry):
        each_way(
            zz,
            lambda o, way: hop(buf.at[o], o, way).wait_send(),
            lambda o: short_hop(o).wait_send(),
        )
        return carry

    lax.fori_loop(0, half, sent, 0)
    tail_hop(across).wait_send()
    total = got[0]
    for t in range(1, tensors):
        total = total + got[t]
    score_ref[...] = total


def per_device_gathered(
    step_input,
    new_kv,
    resp_cache,
    policy_prompt,
    ref_prompt,
    prompt_len,
    resp_len,
    row_owner,
    finished,
    probe,
):
    row_count, step_count, q_width = step_input.shape
    kv_width = new_kv.shape[3]
    q_heads = q_width // HD
    kv_heads = kv_width // HD
    group = q_heads // kv_heads
    peers = lax.axis_size("dp")
    capacity = max(2, (row_count + peers - 1) // peers)
    slots = peers * capacity
    resp_slots = resp_cache.shape[1]
    keys_n = resp_slots + step_count
    width = policy_prompt.shape[1]
    lanes = 2 * group * capacity
    pairs = kv_heads // 2
    dims = (capacity, step_count, resp_slots, width, kv_heads, group)

    tensors = lax.axis_size("tensor")
    vmem = pl.BlockSpec(memory_space=pltpu.VMEM)
    decoded, scores = pl.pallas_call(
        functools.partial(fused_kernel, dims),
        in_specs=[vmem] * 8,
        out_specs=[vmem] * 2,
        out_shape=[
            jax.ShapeDtypeStruct((step_count, row_count, q_width), jnp.bfloat16),
            jax.ShapeDtypeStruct((peers, 8, lanes), jnp.float32),
        ],
        scratch_shapes=[
            pltpu.VMEM((peers, 4 * width + 16, kv_width), jnp.bfloat16),
            pltpu.VMEM((step_count, slots, q_width), jnp.float32),
            pltpu.VMEM((keys_n, 2, slots, kv_width), jnp.float32),
            pltpu.VMEM((step_count, slots, q_width), jnp.float32),
            pltpu.VMEM((2, peers, lanes), jnp.float32),
            pltpu.VMEM((pairs, HD, lanes), jnp.float32),
            pltpu.VMEM((peers, 8, lanes), jnp.float32),
            pltpu.VMEM((tensors, peers, 8, lanes), jnp.float32),
            pltpu.SemaphoreType.DMA((3, peers)),
            pltpu.SemaphoreType.DMA((peers,)),
            pltpu.SemaphoreType.DMA,
            pltpu.SemaphoreType.DMA,
            pltpu.SemaphoreType.DMA((tensors, peers)),
            pltpu.SemaphoreType.DMA((tensors, peers)),
        ],
        compiler_params=pltpu.CompilerParams(
            collective_id=0, has_side_effects=True, vmem_limit_bytes=48 * 1024 * 1024
        ),
    )(
        jnp.transpose(policy_prompt[0], (1, 0, 2)),
        jnp.transpose(ref_prompt[0], (1, 0, 2)),
        jnp.broadcast_to(prompt_len[:, None], (8, HD)),
        jnp.transpose(step_input, (1, 0, 2)),
        jnp.transpose(resp_cache, (1, 2, 0, 3)),
        jnp.transpose(new_kv, (1, 2, 0, 3)),
        jnp.stack([row_owner, resp_len, finished] + [finished] * 5),
        probe.reshape(q_heads, HD),
    )
    decoded_rows = jnp.transpose(decoded, (1, 0, 2))
    scores = scores[:, :step_count].reshape(peers, step_count, 2 * group, capacity)
    scores = jnp.transpose(jnp.sum(scores, axis=2), (0, 2, 1))
    return decoded_rows, scores.reshape(1, slots, step_count)


def per_device(step_input, *rest):
    peers = lax.axis_size("dp")
    rows = step_input.shape[0]
    step_count, q_width = step_input.shape[1:]
    resp_slots, kv_width = rest[1].shape[1], rest[1].shape[3]
    fits = (
        rows == 8 * peers
        and rest[2].shape[1] == HD
        and 16 * q_width == HD * kv_width
        and kv_width % (2 * HD) == 0
        and 8 * (resp_slots + step_count) <= HD
        and peers % 4 == 0
        and step_count <= 8
    )
    if fits:
        return per_device_gathered(step_input, *rest)
    return per_device_routed(step_input, *rest)


def solution(mesh):
    in_specs = (
        P(("groups", "dp"), None, "tensor"),
        P(("groups", "dp"), None, None, "tensor"),
        P(("groups", "dp"), None, None, "tensor"),
        P(("groups", "dp"), None, None, "tensor"),
        P(("groups", "dp"), None, None, "tensor"),
        P(("groups", "dp")),
        P(("groups", "dp")),
        P(("groups", "dp")),
        P(("groups", "dp")),
        P("tensor"),
    )
    out_specs = (P(("groups", "dp"), None, "tensor"), P(("groups", "dp"), None, None))
    return jax.shard_map(
        per_device, mesh=mesh, in_specs=in_specs, out_specs=out_specs, check_vma=False
    )
```
